128 devices in a mesh: row: 8 (over x, core), col: 16 (over z, y).
Axes of the slice: x: 4, y: 4, z: 4, core: 2. Of those that a mesh axis runs over, the one named last changes fastest.
Arguments:
- positions: float32 [3, 8, 1024, 256], P(None, 'row', 'col'), may hold values from -2 to 2
- strengths: float32 [3, 8, 1024, 256], P(None, 'row', 'col'), may hold values from -2 to 2
- live_count: int32 [8, 1024], P('row', 'col'), may hold values from 64 to 256, as said below
- send_list: int32 [8, 16, 16, 16], P('row', 'col'), may hold values from 0 to 63
- partner: int32 [8, 16, 16, 16], P('row', 'col'), may hold values from -1 to 63, as said below
- parent_block: int32 [8, 1024], P('row', 'col'), may hold values from 0 to 255
- parent_cell: int32 [8, 256], P('row'), may hold values from 0 to 63
Outputs:
- force: float32 [3, 8, 1024, 256], P(None, 'row', 'col')
- moments_cell: float32 [12, 8, 256], P(None, 'row', 'col')
- moments_top: float32 [12, 64], replicated
The draws below stay inside these ranges and needn't reach their ends.
Inputs may be any that keep to these rules, and one draw needn't show every extreme that they name: `live_count`: segments at or past a block's live count are padding; some blocks in every draw are full. `partner`: -1 marks an empty slot; for each sender and receiver the used slots come first, and some sender fills all 16 slots to some receiver.
All inputs are finite; a program needn't handle non-finite values.
Results may differ from the reference program's by a relative error of at most 0.00013.
Values sent between devices are 32-bit elements; how exact they have to be, the bound alone decides.
A program may use at most 64 MiB of HBM per device.

```python
import math
import jax
import jax.numpy as jnp
from jax import lax

SEG = 256
BLK_DEV = 64
SLOTS = 16
C2 = 64
BLOCKS_ROW = 1024
C1_SLAB = 256
N_ROW = 8
N_COL = 16


def slot_counts(key):
    drawn = jax.random.randint(key, (N_ROW, N_COL, N_COL), 1, SLOTS + SLOTS // 2 + 1)
    return jnp.minimum(drawn, SLOTS)


def draw_partner(key, part):
    counts = slot_counts(key)
    key = jax.random.fold_in(key, 22)
    picks = jax.random.randint(key, (N_ROW, N_COL, N_COL, SLOTS), 0, BLK_DEV)
    turned = jnp.transpose(counts, (0, 2, 1))
    slot_ids = jnp.arange(SLOTS, dtype=jnp.int32)
    is_used = slot_ids[None, None, None, :] < turned[:, :, :, None]
    return jnp.where(is_used, picks, -1).astype(jnp.int32)


def draw_live_count(key, part):
    key = jax.random.fold_in(key, 23)
    drawn = jax.random.randint(key, (N_ROW, N_COL * BLK_DEV), SEG // 4, SEG + SEG // 4 + 1)
    return jnp.minimum(drawn, SEG).astype(jnp.int32)


def place_ends(result, key, least, top_value):
    shape = result.shape
    index_at = [jax.random.randint(jax.random.fold_in(key, axis), (), 0, shape[axis]) for axis in range(len(shape))]
    result = result.at[tuple(index_at)].set(least)
    longest = shape.index(max(shape))
    index_at[longest] = (index_at[longest] + 1) % shape[longest]
    return result.at[tuple(index_at)].set(top_value)


def level_of(stream_key, dims, shards, smallest, high):
    gain = 1.0
    for dim, shards_of in shards:
        steps = jax.random.uniform(jax.random.fold_in(jax.random.fold_in(stream_key, 6), dim), (shards_of,), jnp.float32, smallest / len(shards), high / len(shards))
        gain = gain * jnp.repeat(jnp.exp(steps), dims[dim] // shards_of).reshape((-1,) + (1,) * (len(dims) - 1 - dim))
    return gain


def bell_draw(stream_key, extent, deviation, bound, cuts=(), held_as=jnp.bfloat16):
    array = jax.random.normal(stream_key, extent, jnp.float32) * deviation
    if len(cuts) > 0:
        array = level_of(stream_key, extent, cuts, -0.22, 0.18) * array
    return jnp.clip(array, min=-bound, max=bound).astype(held_as)


def setup_inputs(seed: int = 0) -> dict:
    arg_keys = jax.random.split(jax.random.key(seed), 8)
    positions = jnp.clip(jax.random.uniform(arg_keys[0], (3, N_ROW, BLOCKS_ROW, SEG), jnp.float32, -2.0, 2.0) * level_of(arg_keys[0], (3, N_ROW, BLOCKS_ROW, SEG), ((1, 8), (2, 16)), -0.4, 0.0), -2.0, 2.0)
    strengths = bell_draw(arg_keys[1], (3, N_ROW, BLOCKS_ROW, SEG), 0.35, 2.0, ((1, 8), (2, 16)), jnp.float32)
    live_count = draw_live_count(jax.random.fold_in(arg_keys[7], 71), 0)
    send_list = place_ends(jax.random.randint(arg_keys[3], (N_ROW, N_COL, N_COL, SLOTS), 0, BLK_DEV), jax.random.fold_in(arg_keys[3], 1), 0, BLK_DEV - 1).astype(jnp.int32)
    partner = draw_partner(jax.random.fold_in(arg_keys[7], 71), 0)
    parent_block = place_ends(jax.random.randint(arg_keys[5], (N_ROW, BLOCKS_ROW), 0, C1_SLAB), jax.random.fold_in(arg_keys[5], 1), 0, C1_SLAB - 1).astype(jnp.int32)
    parent_cell = place_ends(jax.random.randint(arg_keys[6], (N_ROW, C1_SLAB), 0, C2), jax.random.fold_in(arg_keys[6], 1), 0, C2 - 1).astype(jnp.int32)
    return dict(positions=positions, strengths=strengths, live_count=live_count, send_list=send_list, partner=partner, parent_block=parent_block, parent_cell=parent_cell)


CORE_SQUARED = 1.0
MOMENT_UNIT = 0.0625
PRECISE = lax.Precision.HIGHEST

def pair_terms(pos_row, str_row, pos_col, str_col):
    squared = CORE_SQUARED
    coupling = 0.0
    for component in range(3):
        offset = pos_row[:, component, :, None] - pos_col[:, component, None, :]
        squared = squared + offset * offset
        coupling = coupling + str_row[:, component, :, None] * str_col[:, component, None, :]
    weight = coupling / (squared * jnp.sqrt(squared))
    force_row = pos_row * lax.optimization_barrier(jnp.sum(weight, axis=2))[:, None, :] - jnp.einsum('pij,pcj->pci', weight, pos_col, precision=PRECISE)
    force_col = pos_col * lax.optimization_barrier(jnp.sum(weight, axis=1))[:, None, :] - jnp.einsum('pij,pci->pcj', weight, pos_row, precision=PRECISE)
    return (force_row, force_col)

def block_moments(pos_blocks, str_blocks):
    monopole = lax.optimization_barrier(jnp.sum(str_blocks, axis=-1))
    dipole = jnp.einsum('...cs,...ls->...cl', str_blocks, pos_blocks, precision=PRECISE)
    dipole = dipole.reshape(dipole.shape[:-2] + (9,))
    return jnp.concatenate([monopole, dipole], axis=-1) * MOMENT_UNIT

def reference(positions, strengths, live_count, send_list, partner, parent_block, parent_cell):
    blocks_row = N_COL * BLK_DEV
    number = N_ROW * blocks_row
    seg_ids = jnp.arange(SEG, dtype=jnp.int32)
    live_mask = (seg_ids[None, None, :] < live_count[:, :, None]).astype(jnp.float32)
    pos_blocks = jnp.transpose(positions, (1, 2, 0, 3))
    str_blocks = jnp.transpose(strengths, (1, 2, 0, 3)) * live_mask[:, :, None, :]
    flat_pos = pos_blocks.reshape(number, 3, SEG)
    flat_str = str_blocks.reshape(number, 3, SEG)
    row_ids = jnp.arange(N_ROW, dtype=jnp.int32)[:, None, None, None]
    src_ids = jnp.arange(N_COL, dtype=jnp.int32)[None, :, None, None]
    dst_ids = jnp.arange(N_COL, dtype=jnp.int32)[None, None, :, None]
    turned = jnp.transpose(partner, (0, 2, 1, 3))
    is_valid = (turned >= 0).astype(jnp.float32)
    sent_index = row_ids * blocks_row + src_ids * BLK_DEV + send_list
    other_index = row_ids * blocks_row + dst_ids * BLK_DEV + jnp.maximum(turned, 0)
    total_pairs = N_ROW * N_COL * N_COL * SLOTS
    batch_size = math.gcd(total_pairs, 64)
    steps_count = total_pairs // batch_size
    sent_flat = sent_index.reshape(steps_count, batch_size).astype(jnp.int32)
    other_flat = other_index.reshape(steps_count, batch_size).astype(jnp.int32)
    valid_flat = is_valid.reshape(steps_count, batch_size)

    def visit(forces, pair_items):
        sent_ids, other_ids, kept_mask = pair_items
        force_row, force_col = pair_terms(flat_pos[sent_ids], flat_str[sent_ids], flat_pos[other_ids], flat_str[other_ids] * kept_mask[:, None, None])
        forces = forces.at[sent_ids].add(force_row).at[other_ids].add(force_col)
        return (forces, None)
    forces, _ = lax.scan(visit, jnp.zeros((number, 3, SEG), jnp.float32), (sent_flat, other_flat, valid_flat))
    force = jnp.transpose(forces.reshape(N_ROW, blocks_row, 3, SEG), (2, 0, 1, 3))
    moments = block_moments(pos_blocks, str_blocks)
    cell_ids = jnp.arange(C1_SLAB, dtype=jnp.int32)
    cell_hot = (parent_block[:, :, None] == cell_ids[None, None, :]).astype(jnp.float32)
    moments_cell = jnp.einsum('rbm,rbc->mrc', moments, cell_hot, precision=PRECISE)
    top_ids = jnp.arange(C2, dtype=jnp.int32)
    top_hot = (parent_cell[:, :, None] == top_ids[None, None, :]).astype(jnp.float32)
    moments_top = jnp.einsum('mrc,rct->mt', moments_cell, top_hot, precision=PRECISE)
    return (force, moments_cell, moments_top)
```

```python
import functools

import jax
import jax.numpy as jnp
from jax import lax
from jax.experimental import pallas as pl
from jax.experimental.pallas import tpu as pltpu
from jax.sharding import PartitionSpec as P

C2 = 64
CORE_SQUARED = 1.0
MOMENT_UNIT = 0.0625
GROUP = 4
f32, bf16, i32 = jnp.float32, jnp.bfloat16, jnp.int32
MESH = pl.DeviceIdType.MESH


def split3(values):
    high = values.astype(bf16).astype(f32)
    rest = values - high
    middle = rest.astype(bf16).astype(f32)
    return high, middle, rest - middle


def dot(left, right, contract):
    return lax.dot_general(left, right, ((contract[0:1], contract[1:2]), ((), ())), preferred_element_type=f32)


def hot_dot(hot, values, contract=(1, 0)):
    high, middle, low = split3(values)
    return (
        dot(hot, high.astype(bf16), contract)
        + dot(hot, middle.astype(bf16), contract)
        + dot(hot, low.astype(bf16), contract)
    )


def row_ids(shape):
    return lax.broadcasted_iota(i32, shape, 0)


def tile_of(block):
    squares = block[0:1] * block[0:1] + block[1:2] * block[1:2] + block[2:3] * block[2:3]
    return jnp.concatenate([block[0:6], squares, jnp.ones_like(squares)], axis=0)


def distance_features(tile):
    high, middle, low = split3(tile)
    return jnp.concatenate([high, high, high, middle, middle, low], axis=0).astype(bf16)


def distance_coefficients(tile):
    row = row_ids(tile.shape)
    squares = tile[6:7] + CORE_SQUARED
    base = jnp.where(row < 3, -2.0 * tile, jnp.where(row == 7, squares, 0.0))
    high, middle, low = split3(base)
    unit = jnp.where(row == 6, 1.0, 0.0)
    first = jnp.where(row < 3, high, unit)
    second = jnp.where(row < 3, middle, 0.0)
    return jnp.concatenate([high + unit, middle, low, first, second, first], axis=0)


def strength_rows(block):
    width = block.shape[1]
    fours = [jnp.broadcast_to(block[c : c + 1], (4, width)) for c in (3, 4, 5)]
    return jnp.concatenate(fours + [jnp.zeros((4, width), f32)], axis=0)


def charge_features(block):
    one = jnp.ones((1, block.shape[1]), f32)
    four = [one, block[0:3]]
    rows = jnp.concatenate(four * 4, axis=0) * strength_rows(block)
    high = rows.astype(bf16).astype(f32)
    return jnp.concatenate([high, rows - high], axis=0).astype(bf16)


def force_rows(block, sums):
    products = sums * strength_rows(block)
    half = products[0:8] + products[8:16]
    summed = half[0:4] + half[4:8]
    return block[0:3] * summed[0:1] - summed[1:4]


def kernel(
    n_row, n_col, slots,
    send_smem, partner_smem, pos, strength, live, send_vmem, partner_vmem, parent_block, parent_cell,
    force, cell_out, top_out,
    turned, own, coef, charge, sent, received, back, returned, near, highs, lows,
    cell_sent, cell_got, top_sent, top_got, row_sent, row_got,
    sent_sem, received_sem, back_sem, returned_sem, cell_sent_sem, cell_got_sem, top_sent_sem, top_got_sem,
    row_sent_sem, row_got_sem,
):
    blocks, width = pos.shape[1], pos.shape[2]
    share = cell_got.shape[1]
    groups = slots // GROUP
    my_row, me = lax.axis_index("row"), lax.axis_index("col")

    barrier = pltpu.get_barrier_semaphore()

    def greet_col(step, carry):
        pl.semaphore_signal(barrier, inc=1, device_id={"col": lax.rem(me + step, n_col)}, device_id_type=MESH)
        return carry

    def greet_row(step, carry):
        pl.semaphore_signal(barrier, inc=1, device_id={"row": lax.rem(my_row + step, n_row)}, device_id_type=MESH)
        return carry

    lax.fori_loop(1, n_col, greet_col, 0)
    lax.fori_loop(1, n_row, greet_row, 0)

    same = row_ids((blocks, blocks)) == lax.broadcasted_iota(i32, (blocks, blocks), 1)
    counts = jnp.sum(jnp.where(same, live[...], 0).astype(f32), axis=1, keepdims=True)
    lane = lax.broadcasted_iota(i32, (blocks, width), 1).astype(f32)
    mask = jnp.where(lane < counts, 1.0, 0.0)
    x = [pos[c] for c in range(3)]
    q = [strength[c] * mask for c in range(3)]
    squares = x[0] * x[0] + x[1] * x[1] + x[2] * x[2]
    for c, rows in enumerate(x + q + [squares, jnp.ones_like(squares)]):
        for part in range(width // 128):
            turned[part, pl.ds(c, blocks, stride=8), :] = rows[:, part * 128 : part * 128 + 128]
    for part in range(width // 128):
        own[:, :, part * 128 : part * 128 + 128] = turned[part].reshape(blocks, 8, 128)

    def own_block(index):
        return own[index]

    def gather_to(target, receiver):
        for k in range(slots):
            target[receiver, k] = own_block(send_smem[receiver, k])[0:6]

    gather_to(received, me)
    pl.semaphore_wait(barrier, n_col + n_row - 2)

    def send_copy(peer):
        return pltpu.make_async_remote_copy(
            src_ref=sent.at[peer], dst_ref=received.at[me], send_sem=sent_sem.at[peer],
            recv_sem=received_sem.at[me], device_id={"col": peer}, device_id_type=MESH)

    def arrival(peer):
        return pltpu.make_async_remote_copy(
            src_ref=sent.at[peer], dst_ref=received.at[peer], send_sem=sent_sem.at[peer],
            recv_sem=received_sem.at[peer], device_id={"col": peer}, device_id_type=MESH)

    def back_copy(peer):
        return pltpu.make_async_remote_copy(
            src_ref=back.at[peer], dst_ref=returned.at[me], send_sem=back_sem.at[peer],
            recv_sem=returned_sem.at[me], device_id={"col": peer}, device_id_type=MESH)

    def back_arrival(peer):
        return pltpu.make_async_remote_copy(
            src_ref=back.at[peer], dst_ref=returned.at[peer], send_sem=back_sem.at[peer],
            recv_sem=returned_sem.at[peer], device_id={"col": peer}, device_id_type=MESH)

    def cell_copy(peer, at):
        return pltpu.make_async_remote_copy(
            src_ref=cell_sent.at[peer], dst_ref=cell_got.at[at], send_sem=cell_sent_sem.at[peer],
            recv_sem=cell_got_sem.at[at], device_id={"col": peer}, device_id_type=MESH)

    def top_copy(peer, at):
        return pltpu.make_async_remote_copy(
            src_ref=top_sent, dst_ref=top_got.at[at], send_sem=top_sent_sem.at[peer],
            recv_sem=top_got_sem.at[at], device_id={"col": peer}, device_id_type=MESH)

    def row_copy(peer, at):
        return pltpu.make_async_remote_copy(
            src_ref=row_sent, dst_ref=row_got.at[at], send_sem=row_sent_sem.at[peer],
            recv_sem=row_got_sem.at[at], device_id={"row": peer}, device_id_type=MESH)

    def send_step(step, carry):
        peer = lax.rem(me + n_col - step, n_col)
        gather_to(sent, peer)
        send_copy(peer).start()
        return carry

    lax.fori_loop(1, n_col, send_step, 0)

    columns = lax.broadcasted_iota(i32, (blocks, 128), 1)
    moments = jnp.zeros((blocks, 128), f32)
    terms = q + [q[c] * x[l] for c in range(3) for l in range(3)]
    for m, term in enumerate(terms):
        moments = jnp.where(columns == m, jnp.sum(term, axis=1, keepdims=True), moments)
    moments = moments * MOMENT_UNIT
    cells = n_col * share
    cell_hot = jnp.where(row_ids((cells, blocks)) == parent_block[...], 1.0, 0.0).astype(bf16)
    cell_part = hot_dot(cell_hot, moments)
    cell_sent[...] = cell_part.reshape(n_col, share, 128)
    cell_got[me] = cell_sent[me]
    top_hot = jnp.where(row_ids((C2, cells)) == parent_cell[...], 1.0, 0.0).astype(bf16)
    top_part = hot_dot(top_hot, cell_part)
    padded = jnp.concatenate([top_part, jnp.zeros((128 - C2, 128), f32)], axis=0)
    top_sent[...] = jnp.transpose(padded)[0:16]
    top_got[me] = top_sent[...]

    def moment_step(step, carry):
        peer = lax.rem(me + n_col - step, n_col)
        cell_copy(peer, me).start()
        top_copy(peer, me).start()
        return carry

    lax.fori_loop(1, n_col, moment_step, 0)

    def prepare(block, carry):
        tile = own_block(block)
        coef[block] = jnp.transpose(distance_coefficients(tile)).astype(bf16)
        charge[block] = charge_features(tile)
        return carry

    lax.fori_loop(0, blocks, prepare, 0)

    def partner_of(sender, k):
        return jnp.maximum(partner_smem[sender, k], 0)

    def compute(sender, group, slot):
        for u in range(GROUP):
            k = group * GROUP + u
            features = distance_features(tile_of(received[sender, k]))
            squared = dot(coef[partner_of(sender, k)], features, (1, 0))
            inverse = lax.rsqrt(squared)
            cubed = inverse * inverse * inverse
            high = cubed.astype(bf16)
            highs[slot, u] = high
            lows[slot, u] = (cubed - high.astype(f32)).astype(bf16)

    def use(sender, group, slot):
        for u in range(GROUP):
            k = group * GROUP + u
            near_at = partner_of(sender, k)
            block = received[sender, k]
            high, low = highs[slot, u], lows[slot, u]
            own_charge = charge[near_at]
            sums = dot(own_charge, high, (1, 0))
            sums = sums[0:16] + sums[16:32] + dot(own_charge[0:16], low, (1, 0))
            valid = jnp.clip(partner_smem[sender, k] + 1, 0, 1).astype(f32)
            rows = force_rows(block, sums) * valid
            for l in range(3):
                back[sender, l, k : k + 1] = rows[l : l + 1]
            far_charge = charge_features(block)
            sums = dot(far_charge, high, (1, 1))
            sums = sums[0:16] + sums[16:32] + dot(far_charge[0:16], low, (1, 1))
            rows = force_rows(own_block(near_at), sums)
            for l in range(3):
                near[l, sender, k : k + 1] = rows[l : l + 1]

    def sum_of(got, count):
        total = got[0]
        for at in range(1, count):
            total = total + got[at]
        return total

    compute(me, 0, 0)

    def sender_step(step, carry):
        sender = lax.rem(me + step, n_col)
        following = lax.rem(me + step + 1, n_col)
        for group in range(groups - 1):
            compute(sender, group + 1, (group + 1) % 2)
            use(sender, group, group % 2)

        @pl.when(step < n_col - 1)
        def _():
            arrival(following).wait_recv()

        compute(following, 0, 0)
        use(sender, groups - 1, (groups - 1) % 2)

        @pl.when(step > 0)
        def _():
            back_copy(sender).start()

        @pl.when(step == 4)
        def _():
            def wait_moments(other, inner):
                peer = lax.rem(me + other, n_col)
                cell_copy(peer, peer).wait_recv()
                top_copy(peer, peer).wait_recv()
                return inner

            lax.fori_loop(1, n_col, wait_moments, 0)
            cell_sum = sum_of(cell_got, n_col)
            cell_rows = jnp.concatenate([cell_sum, jnp.zeros((128 - share, 128), f32)], axis=0)
            cell_out[...] = jnp.transpose(cell_rows)[0:12, 0:share]
            row_sent[...] = sum_of(top_got, n_col)
            row_got[my_row] = row_sent[...]

            def row_step(other, inner):
                row_copy(lax.rem(my_row + other, n_row), my_row).start()
                return inner

            lax.fori_loop(1, n_row, row_step, 0)

        return carry

    lax.fori_loop(0, n_col, sender_step, 0)

    returned[me] = back[me]

    def row_wait(other, carry):
        peer = lax.rem(my_row + other, n_row)
        row_copy(peer, peer).wait_recv()
        return carry

    lax.fori_loop(1, n_row, row_wait, 0)
    top_out[...] = sum_of(row_got, n_row)[0:12, 0:C2]

    pairs = n_col * slots
    pair = lax.broadcasted_iota(i32, (slots, pairs), 1)
    pair_row = row_ids((slots, pairs))
    in_slot = jnp.where(lax.rem(pair, slots) == pair_row, 1.0, 0.0).astype(bf16)
    pair_c = lax.broadcasted_iota(i32, (n_col, pairs), 1)
    in_peer = jnp.where(lax.div(pair_c, slots) == row_ids((n_col, pairs)), 1.0, 0.0)
    block_id = row_ids((blocks, pairs)).astype(f32)

    def hot_of(listed):
        spread = dot(listed[...].astype(f32).astype(bf16), in_slot, (1, 0))
        flat = jnp.sum(spread * in_peer, axis=0, keepdims=True)
        return jnp.where(block_id == flat, 1.0, 0.0).astype(bf16)

    near_hot = hot_of(partner_vmem)
    totals = [hot_dot(near_hot, near[l].reshape(pairs, width)) for l in range(3)]
    sent_hot = hot_of(send_vmem)

    def finish(step, carry):
        peer = lax.rem(me + step, n_col)
        back_arrival(peer).wait_recv()
        return carry

    lax.fori_loop(1, n_col, finish, 0)
    for l in range(3):
        force[l] = totals[l] + hot_dot(sent_hot, returned[:, l].reshape(pairs, width))

    def drain(step, carry):
        peer = lax.rem(me + step, n_col)
        send_copy(peer).wait_send()
        back_copy(peer).wait_send()
        cell_copy(peer, me).wait_send()
        top_copy(peer, me).wait_send()
        return carry

    lax.fori_loop(1, n_col, drain, 0)

    def drain_row(step, carry):
        row_copy(lax.rem(my_row + step, n_row), my_row).wait_send()
        return carry

    lax.fori_loop(1, n_row, drain_row, 0)


def body(positions, strengths, live_count, send_list, partner, parent_block, parent_cell):
    n_row, n_col = lax.axis_size("row"), lax.axis_size("col")
    blocks, width = positions.shape[2:]
    slots = send_list.shape[3]
    cells = parent_cell.shape[1]
    share = cells // n_col
    vmem = pl.BlockSpec(memory_space=pltpu.VMEM)
    smem = pl.BlockSpec(memory_space=pltpu.SMEM)
    dma = pltpu.SemaphoreType.DMA
    sends, partners = send_list[0, 0], partner[0, 0]
    force, cell, top = pl.pallas_call(
        functools.partial(kernel, n_row, n_col, slots),
        out_shape=(
            jax.ShapeDtypeStruct((3, blocks, width), f32),
            jax.ShapeDtypeStruct((12, share), f32),
            jax.ShapeDtypeStruct((12, C2), f32),
        ),
        in_specs=[smem, smem] + [vmem] * 7,
        out_specs=(vmem, vmem, vmem),
        scratch_shapes=[
            pltpu.VMEM((width // 128, blocks * 8, 128), f32),
            pltpu.VMEM((blocks, 8, width), f32),
            pltpu.VMEM((blocks, width, 48), bf16),
            pltpu.VMEM((blocks, 32, width), bf16),
            pltpu.VMEM((n_col, slots, 6, width), f32),
            pltpu.VMEM((n_col, slots, 6, width), f32),
            pltpu.VMEM((n_col, 3, slots, width), f32),
            pltpu.VMEM((n_col, 3, slots, width), f32),
            pltpu.VMEM((3, n_col, slots, width), f32),
            pltpu.VMEM((2, GROUP, width, width), bf16),
            pltpu.VMEM((2, GROUP, width, width), bf16),
            pltpu.VMEM((n_col, share, 128), f32),
            pltpu.VMEM((n_col, share, 128), f32),
            pltpu.VMEM((16, 128), f32),
            pltpu.VMEM((n_col, 16, 128), f32),
            pltpu.VMEM((16, 128), f32),
            pltpu.VMEM((n_row, 16, 128), f32),
            *[dma((n_col,)) for _ in range(8)],
            dma((n_row,)),
            dma((n_row,)),
        ],
        compiler_params=pltpu.CompilerParams(
            collective_id=0, has_side_effects=True, vmem_limit_bytes=40 * 1024 * 1024
        ),
        name="pair_forces",
    )(sends, partners, positions[:, 0], strengths[:, 0], live_count, sends, partners, parent_block, parent_cell)
    return force[:, None], cell[:, None, :], top


def solution(mesh):
    placed = (
        P(None, "row", "col", None),
        P(None, "row", "col", None),
        P("row", "col"),
        P("row", "col", None, None),
        P("row", "col", None, None),
        P("row", "col"),
        P("row", None),
    )
    return jax.shard_map(
        body,
        mesh=mesh,
        in_specs=placed,
        out_specs=(P(None, "row", "col", None), P(None, "row", "col"), P()),
        check_vma=False,
    )
```

```python
import functools

import jax
import jax.numpy as jnp
from jax import lax
from jax.experimental import pallas as pl
from jax.experimental.pallas import tpu as pltpu
from jax.sharding import PartitionSpec as P

C2 = 64
CORE_SQUARED = 1.0
MOMENT_UNIT = 0.0625
GROUP = 4
AHEAD = 6
LINES = 6
CHUNKS = 1
PREPARED = 8
RING = 4
OFFSETS = (
    (0, 1), (0, 3), (1, 0), (3, 0), (1, 1), (3, 3), (1, 3), (3, 1),
    (0, 2), (2, 0), (2, 1), (2, 3), (1, 2), (3, 2), (2, 2),
)
CODE_Z = sum(offset[0] * RING**step for step, offset in enumerate(OFFSETS))
CODE_Y = sum(offset[1] * RING**step for step, offset in enumerate(OFFSETS))
f32, bf16, i32 = jnp.float32, jnp.bfloat16, jnp.int32
MESH = pl.DeviceIdType.MESH


def split3(values):
    high = values.astype(bf16).astype(f32)
    rest = values - high
    middle = rest.astype(bf16).astype(f32)
    return high, middle, rest - middle


def dot(left, right, contract):
    return lax.dot_general(left, right, ((contract[0:1], contract[1:2]), ((), ())), preferred_element_type=f32)


def hot_dot(hot, values, contract=(1, 0)):
    high, middle, low = split3(values)
    return (
        dot(hot, high.astype(bf16), contract)
        + dot(hot, middle.astype(bf16), contract)
        + dot(hot, low.astype(bf16), contract)
    )


def row_ids(shape):
    return lax.broadcasted_iota(i32, shape, 0)


def tile_of(block):
    squares = block[0:1] * block[0:1] + block[1:2] * block[1:2] + block[2:3] * block[2:3]
    return jnp.concatenate([block[0:6], squares, jnp.ones_like(squares)], axis=0)


def distance_features(tile):
    high, middle, low = split3(tile)
    return jnp.concatenate([high, high, high, middle, middle, low], axis=0).astype(bf16)


def distance_coefficients(tile):
    row = row_ids(tile.shape)
    squares = tile[6:7] + CORE_SQUARED
    base = jnp.where(row < 3, -2.0 * tile, jnp.where(row == 7, squares, 0.0))
    high, middle, low = split3(base)
    unit = jnp.where(row == 6, 1.0, 0.0)
    first = jnp.where(row < 3, high, unit)
    second = jnp.where(row < 3, middle, 0.0)
    return jnp.concatenate([high + unit, middle, low, first, second, first], axis=0)


def strength_rows(block):
    width = block.shape[1]
    fours = [jnp.broadcast_to(block[c : c + 1], (4, width)) for c in (3, 4, 5)]
    return jnp.concatenate(fours + [jnp.zeros((4, width), f32)], axis=0)


def charge_features(block):
    one = jnp.ones((1, block.shape[1]), f32)
    four = [one, block[0:3]]
    rows = jnp.concatenate(four * 4, axis=0) * strength_rows(block)
    high = rows.astype(bf16).astype(f32)
    return jnp.concatenate([high, rows - high], axis=0).astype(bf16)


def force_rows(block, sums):
    products = sums * strength_rows(block)
    half = products[0:8] + products[8:16]
    summed = half[0:4] + half[4:8]
    return block[0:3] * summed[0:1] - summed[1:4]


def kernel(
    n_row, n_col, slots,
    pos_in, strength_in, live_in, send_in, partner_in, parent_block_in, parent_cell_in,
    force, cell_out, top_out,
    pos, strength, live, send_smem, partner_smem, send_vmem, partner_vmem, parent_block, parent_cell, turned, own, coef, charge, sent, received, back, returned, near, highs, lows,
    cell_sent, cell_got, top_sent, top_got, row_sent, row_got,
    sent_sem, received_sem, back_sem, returned_sem, cell_sent_sem, cell_got_sem, top_sent_sem, top_got_sem,
    row_sent_sem, row_got_sem, input_sem,
):
    moves = (
        (live_in, live), (pos_in, pos), (strength_in, strength), (send_in, send_smem), (partner_in, partner_smem),
        (send_in, send_vmem), (partner_in, partner_vmem), (parent_block_in, parent_block), (parent_cell_in, parent_cell),
    )
    inputs = [pltpu.make_async_copy(a, b, input_sem.at[at]) for at, (a, b) in enumerate(moves)]
    for copy in inputs:
        copy.start()
    blocks, width = pos.shape[1], pos.shape[2]
    share = cell_got.shape[1]
    groups = slots // GROUP
    my_row, me = lax.axis_index("row"), lax.axis_index("col")

    my_z, my_y = lax.div(me, RING), lax.rem(me, RING)

    def source(code):
        return lax.rem(my_z + lax.rem(code[0], RING), RING) * RING + lax.rem(my_y + lax.rem(code[1], RING), RING)

    def target(code):
        z = lax.rem(my_z + RING - lax.rem(code[0], RING), RING)
        return z * RING + lax.rem(my_y + RING - lax.rem(code[1], RING), RING)

    def next_code(code):
        return lax.div(code[0], RING), lax.div(code[1], RING)

    barrier = pltpu.get_barrier_semaphore()

    def greet_col(step, carry):
        pl.semaphore_signal(barrier, inc=1, device_id={"col": lax.rem(me + step, n_col)}, device_id_type=MESH)
        return carry

    def greet_row(step, carry):
        pl.semaphore_signal(barrier, inc=1, device_id={"row": lax.rem(my_row + step, n_row)}, device_id_type=MESH)
        return carry

    lax.fori_loop(1, n_col, greet_col, 0)
    lax.fori_loop(1, n_row, greet_row, 0)

    for copy in inputs:
        copy.wait()

    same = row_ids((blocks, blocks)) == lax.broadcasted_iota(i32, (blocks, blocks), 1)
    counts = jnp.sum(jnp.where(same, live[...], 0).astype(f32), axis=1, keepdims=True)
    lane = lax.broadcasted_iota(i32, (blocks, width), 1).astype(f32)
    mask = jnp.where(lane < counts, 1.0, 0.0)
    x = [pos[c] for c in range(3)]
    q = [strength[c] * mask for c in range(3)]
    squares = x[0] * x[0] + x[1] * x[1] + x[2] * x[2]
    for c, rows in enumerate(x + q + [squares, jnp.ones_like(squares)]):
        for part in range(width // 128):
            turned[part, pl.ds(c, blocks, stride=8), :] = rows[:, part * 128 : part * 128 + 128]
    for part in range(width // 128):
        own[:, :, part * 128 : part * 128 + 128] = turned[part].reshape(blocks, 8, 128)

    def own_block(index):
        return own[index]

    def gather_to(buffer, receiver):
        for k in range(slots):
            buffer[receiver, LINES * k : LINES * k + LINES] = own_block(send_smem[receiver, k])[0:LINES]

    gather_to(received, me)
    pl.semaphore_wait(barrier, n_col + n_row - 2)

    def send_copy(peer):
        return pltpu.make_async_remote_copy(
            src_ref=sent.at[peer], dst_ref=received.at[me], send_sem=sent_sem.at[peer],
            recv_sem=received_sem.at[me], device_id={"col": peer}, device_id_type=MESH)

    def start_send(peer):
        part = slots * LINES // CHUNKS
        for chunk in range(CHUNKS):
            lines = pl.ds(chunk * part, part)
            pltpu.make_async_remote_copy(
                src_ref=sent.at[peer, lines], dst_ref=received.at[me, lines], send_sem=sent_sem.at[peer],
                recv_sem=received_sem.at[me], device_id={"col": peer}, device_id_type=MESH).start()

    def arrival(peer):
        return pltpu.make_async_remote_copy(
            src_ref=sent.at[peer], dst_ref=received.at[peer], send_sem=sent_sem.at[peer],
            recv_sem=received_sem.at[peer], device_id={"col": peer}, device_id_type=MESH)

    def back_copy(peer):
        return pltpu.make_async_remote_copy(
            src_ref=back.at[peer], dst_ref=returned.at[me], send_sem=back_sem.at[peer],
            recv_sem=returned_sem.at[me], device_id={"col": peer}, device_id_type=MESH)

    def back_arrival(peer):
        return pltpu.make_async_remote_copy(
            src_ref=back.at[peer], dst_ref=returned.at[peer], send_sem=back_sem.at[peer],
            recv_sem=returned_sem.at[peer], device_id={"col": peer}, device_id_type=MESH)

    def cell_copy(peer, at):
        return pltpu.make_async_remote_copy(
            src_ref=cell_sent.at[peer], dst_ref=cell_got.at[at], send_sem=cell_sent_sem.at[peer],
            recv_sem=cell_got_sem.at[at], device_id={"col": peer}, device_id_type=MESH)

    def top_copy(peer, at):
        return pltpu.make_async_remote_copy(
            src_ref=top_sent, dst_ref=top_got.at[at], send_sem=top_sent_sem.at[peer],
            recv_sem=top_got_sem.at[at], device_id={"col": peer}, device_id_type=MESH)

    def row_copy(peer, at):
        return pltpu.make_async_remote_copy(
            src_ref=row_sent, dst_ref=row_got.at[at], send_sem=row_sent_sem.at[peer],
            recv_sem=row_got_sem.at[at], device_id={"row": peer}, device_id_type=MESH)

    def send_step(step, code):
        peer = target(code)
        gather_to(sent, peer)
        start_send(peer)
        return next_code(code)

    codes = (jnp.int32(CODE_Z), jnp.int32(CODE_Y))
    send_code = lax.fori_loop(0, AHEAD, send_step, codes)

    def prepare(step, carry):
        for u in range(PREPARED):
            block = step * PREPARED + u
            tile = own_block(block)
            coef[block] = jnp.transpose(distance_coefficients(tile)).astype(bf16)
            charge[block] = charge_features(tile)
        return carry

    lax.fori_loop(0, blocks // PREPARED, prepare, 0)

    columns = lax.broadcasted_iota(i32, (blocks, 128), 1)
    moments = jnp.zeros((blocks, 128), f32)
    terms = q + [q[c] * x[l] for c in range(3) for l in range(3)]
    for m, term in enumerate(terms):
        moments = jnp.where(columns == m, jnp.sum(term, axis=1, keepdims=True), moments)
    moments = moments * MOMENT_UNIT
    cells = n_col * share
    cell_hot = jnp.where(row_ids((cells, blocks)) == parent_block[...], 1.0, 0.0).astype(bf16)
    cell_part = hot_dot(cell_hot, moments)
    cell_sent[...] = cell_part.reshape(n_col, share, 128)
    cell_got[me] = cell_sent[me]
    top_hot = jnp.where(row_ids((C2, cells)) == parent_cell[...], 1.0, 0.0).astype(bf16)
    top_part = hot_dot(top_hot, cell_part)
    padded = jnp.concatenate([top_part, jnp.zeros((128 - C2, 128), f32)], axis=0)
    top_sent[...] = jnp.transpose(padded)[0:16]
    top_got[me] = top_sent[...]

    def moment_step(step, carry):
        peer = lax.rem(me + n_col - step, n_col)
        cell_copy(peer, me).start()
        top_copy(peer, me).start()
        return carry

    lax.fori_loop(1, n_col, moment_step, 0)

    def partner_of(sender, k):
        return jnp.maximum(partner_smem[sender, k], 0)

    def compute(sender, group, slot):
        for u in range(GROUP):
            k = group * GROUP + u
            features = distance_features(tile_of(received[sender, LINES * k : LINES * k + LINES]))
            squared = dot(coef[partner_of(sender, k)], features, (1, 0))
            inverse = lax.rsqrt(squared)
            cubed = inverse * inverse * inverse
            high = cubed.astype(bf16)
            highs[slot, u] = high
            lows[slot, u] = (cubed - high.astype(f32)).astype(bf16)

    def use(sender, group, slot):
        for u in range(GROUP):
            k = group * GROUP + u
            near_at = partner_of(sender, k)
            block = received[sender, LINES * k : LINES * k + LINES]
            high, low = highs[slot, u], lows[slot, u]
            own_charge = charge[near_at]
            sums = dot(own_charge, high, (1, 0))
            sums = sums[0:16] + sums[16:32] + dot(own_charge[0:16], low, (1, 0))
            valid = jnp.clip(partner_smem[sender, k] + 1, 0, 1).astype(f32)
            rows = force_rows(block, sums) * valid
            for l in range(3):
                back[sender, l, k : k + 1] = rows[l : l + 1]
            far_charge = charge_features(block)
            sums = dot(far_charge, high, (1, 1))
            sums = sums[0:16] + sums[16:32] + dot(far_charge[0:16], low, (1, 1))
            rows = force_rows(own_block(near_at), sums)
            for l in range(3):
                near[l, sender, k : k + 1] = rows[l : l + 1]

    def sum_of(got, count):
        total = got[0]
        for at in range(1, count):
            total = total + got[at]
        return total

    first = source(codes)
    arrival(first).wait_recv()
    compute(first, 0, 0)

    def sender_step(step, carry):
        code, send_code = carry[0:2], carry[2:4]
        sender = source(code)
        following_code = next_code(code)
        following = source(following_code)

        @pl.when(step + AHEAD < n_col - 1)
        def _():
            send_step(step, send_code)

        for group in range(groups - 1):
            compute(sender, group + 1, (group + 1) % 2)
            use(sender, group, group % 2)

        @pl.when(step < n_col - 2)
        def _():
            arrival(following).wait_recv()

        compute(following, 0, 0)
        use(sender, groups - 1, (groups - 1) % 2)

        @pl.when(step < n_col - 1)
        def _():
            back_copy(sender).start()

        @pl.when(step == 4)
        def _():
            def wait_moments(other, inner):
                peer = lax.rem(me + other, n_col)
                cell_copy(peer, peer).wait_recv()
                top_copy(peer, peer).wait_recv()
                return inner

            lax.fori_loop(1, n_col, wait_moments, 0)
            cell_sum = sum_of(cell_got, n_col)
            cell_rows = jnp.concatenate([cell_sum, jnp.zeros((128 - share, 128), f32)], axis=0)
            cell_out[...] = jnp.transpose(cell_rows)[0:12, 0:share]
            row_sent[...] = sum_of(top_got, n_col)
            row_got[my_row] = row_sent[...]

            def row_step(other, inner):
                row_copy(lax.rem(my_row + other, n_row), my_row).start()
                return inner

            lax.fori_loop(1, n_row, row_step, 0)

        return following_code + next_code(send_code)

    lax.fori_loop(0, n_col, sender_step, codes + send_code)

    returned[me] = back[me]

    def row_wait(other, carry):
        peer = lax.rem(my_row + other, n_row)
        row_copy(peer, peer).wait_recv()
        return carry

    lax.fori_loop(1, n_row, row_wait, 0)
    top_out[...] = sum_of(row_got, n_row)[0:12, 0:C2]

    pairs = n_col * slots
    pair = lax.broadcasted_iota(i32, (slots, pairs), 1)
    pair_row = row_ids((slots, pairs))
    in_slot = jnp.where(lax.rem(pair, slots) == pair_row, 1.0, 0.0).astype(bf16)
    pair_c = lax.broadcasted_iota(i32, (n_col, pairs), 1)
    in_peer = jnp.where(lax.div(pair_c, slots) == row_ids((n_col, pairs)), 1.0, 0.0)
    block_id = row_ids((blocks, pairs)).astype(f32)

    def hot_of(listed):
        spread = dot(listed[...].astype(f32).astype(bf16), in_slot, (1, 0))
        flat = jnp.sum(spread * in_peer, axis=0, keepdims=True)
        return jnp.where(block_id == flat, 1.0, 0.0).astype(bf16)

    near_hot = hot_of(partner_vmem)
    totals = [hot_dot(near_hot, near[l].reshape(pairs, width)) for l in range(3)]
    sent_hot = hot_of(send_vmem)

    def finish(step, carry):
        peer = lax.rem(me + step, n_col)
        back_arrival(peer).wait_recv()
        return carry

    lax.fori_loop(1, n_col, finish, 0)
    for l in range(3):
        force[l] = totals[l] + hot_dot(sent_hot, returned[:, l].reshape(pairs, width))

    def drain(step, carry):
        peer = lax.rem(me + step, n_col)
        send_copy(peer).wait_send()
        back_copy(peer).wait_send()
        cell_copy(peer, me).wait_send()
        top_copy(peer, me).wait_send()
        return carry

    lax.fori_loop(1, n_col, drain, 0)

    def drain_row(step, carry):
        row_copy(lax.rem(my_row + step, n_row), my_row).wait_send()
        return carry

    lax.fori_loop(1, n_row, drain_row, 0)


def body(positions, strengths, live_count, send_list, partner, parent_block, parent_cell):
    n_row, n_col = lax.axis_size("row"), lax.axis_size("col")
    blocks, width = positions.shape[2:]
    slots = send_list.shape[3]
    cells = parent_cell.shape[1]
    share = cells // n_col
    vmem = pl.BlockSpec(memory_space=pltpu.VMEM)
    hbm = pl.BlockSpec(memory_space=pl.ANY)
    dma = pltpu.SemaphoreType.DMA
    force, cell, top = pl.pallas_call(
        functools.partial(kernel, n_row, n_col, slots),
        out_shape=(
            jax.ShapeDtypeStruct((3, blocks, width), f32),
            jax.ShapeDtypeStruct((12, share), f32),
            jax.ShapeDtypeStruct((12, C2), f32),
        ),
        in_specs=[hbm] * 7,
        out_specs=(vmem, vmem, vmem),
        scratch_shapes=[
            pltpu.VMEM((3, blocks, width), f32),
            pltpu.VMEM((3, blocks, width), f32),
            pltpu.VMEM((1, blocks), i32),
            pltpu.SMEM((n_col, slots), i32),
            pltpu.SMEM((n_col, slots), i32),
            pltpu.VMEM((n_col, slots), i32),
            pltpu.VMEM((n_col, slots), i32),
            pltpu.VMEM((1, blocks), i32),
            pltpu.VMEM((1, cells), i32),
            pltpu.VMEM((width // 128, blocks * 8, 128), f32),
            pltpu.VMEM((blocks, 8, width), f32),
            pltpu.VMEM((blocks, width, 48), bf16),
            pltpu.VMEM((blocks, 32, width), bf16),
            pltpu.VMEM((n_col, slots * LINES, width), f32),
            pltpu.VMEM((n_col, slots * LINES, width), f32),
            pltpu.VMEM((n_col, 3, slots, width), f32),
            pltpu.VMEM((n_col, 3, slots, width), f32),
            pltpu.VMEM((3, n_col, slots, width), f32),
            pltpu.VMEM((2, GROUP, width, width), bf16),
            pltpu.VMEM((2, GROUP, width, width), bf16),
            pltpu.VMEM((n_col, share, 128), f32),
            pltpu.VMEM((n_col, share, 128), f32),
            pltpu.VMEM((16, 128), f32),
            pltpu.VMEM((n_col, 16, 128), f32),
            pltpu.VMEM((16, 128), f32),
            pltpu.VMEM((n_row, 16, 128), f32),
            *[dma((n_col,)) for _ in range(8)],
            dma((n_row,)),
            dma((n_row,)),
            dma((9,)),
        ],
        compiler_params=pltpu.CompilerParams(
            collective_id=0, has_side_effects=True, vmem_limit_bytes=40 * 1024 * 1024
        ),
        name="pair_forces",
    )(positions[:, 0], strengths[:, 0], live_count, send_list[0, 0], partner[0, 0], parent_block, parent_cell)
    return force[:, None], cell[:, None, :], top


def solution(mesh):
    placed = (
        P(None, "row", "col", None),
        P(None, "row", "col", None),
        P("row", "col"),
        P("row", "col", None, None),
        P("row", "col", None, None),
        P("row", "col"),
        P("row", None),
    )
    return jax.shard_map(
        body,
        mesh=mesh,
        in_specs=placed,
        out_specs=(P(None, "row", "col", None), P(None, "row", "col"), P()),
        check_vma=False,
    )
```

```python
import functools

import jax
import jax.numpy as jnp
from jax import lax
from jax.experimental import pallas as pl
from jax.experimental.pallas import tpu as pltpu
from jax.sharding import PartitionSpec as P

C2 = 64
CORE_SQUARED = 1.0
MOMENT_UNIT = 0.0625
GROUP = 4
AHEAD = 6
LINES = 6
CHUNKS = 1
PREPARED = 8
RING = 4
OFFSETS = (
    (0, 1), (0, 3), (1, 0), (3, 0), (1, 1), (3, 3), (1, 3), (3, 1),
    (0, 2), (2, 0), (2, 1), (2, 3), (1, 2), (3, 2), (2, 2),
)
CODE_Z = sum(offset[0] * RING**step for step, offset in enumerate(OFFSETS))
CODE_Y = sum(offset[1] * RING**step for step, offset in enumerate(OFFSETS))
f32, bf16, i32 = jnp.float32, jnp.bfloat16, jnp.int32
MESH = pl.DeviceIdType.MESH


def split3(values):
    high = values.astype(bf16).astype(f32)
    rest = values - high
    middle = rest.astype(bf16).astype(f32)
    return high, middle, rest - middle


def dot(left, right, contract):
    return lax.dot_general(left, right, ((contract[0:1], contract[1:2]), ((), ())), preferred_element_type=f32)


def hot_dot(hot, values, contract=(1, 0)):
    high, middle, low = split3(values)
    return (
        dot(hot, high.astype(bf16), contract)
        + dot(hot, middle.astype(bf16), contract)
        + dot(hot, low.astype(bf16), contract)
    )


def row_ids(shape):
    return lax.broadcasted_iota(i32, shape, 0)


def tile_of(block):
    squares = block[0:1] * block[0:1] + block[1:2] * block[1:2] + block[2:3] * block[2:3]
    return jnp.concatenate([block[0:6], squares, jnp.ones_like(squares)], axis=0)


def distance_features(tile):
    high, middle, low = split3(tile)
    return jnp.concatenate([high, high, high, middle, middle, low], axis=0).astype(bf16)


def distance_coefficients(tile):
    row = row_ids(tile.shape)
    squares = tile[6:7] + CORE_SQUARED
    base = jnp.where(row < 3, -2.0 * tile, jnp.where(row == 7, squares, 0.0))
    high, middle, low = split3(base)
    unit = jnp.where(row == 6, 1.0, 0.0)
    first = jnp.where(row < 3, high, unit)
    second = jnp.where(row < 3, middle, 0.0)
    return jnp.concatenate([high + unit, middle, low, first, second, first], axis=0)


def strength_rows(block):
    width = block.shape[1]
    fours = [jnp.broadcast_to(block[c : c + 1], (4, width)) for c in (3, 4, 5)]
    return jnp.concatenate(fours + [jnp.zeros((4, width), f32)], axis=0)


def charge_features(block):
    one = jnp.ones((1, block.shape[1]), f32)
    four = [one, block[0:3]]
    rows = jnp.concatenate(four * 4, axis=0) * strength_rows(block)
    high = rows.astype(bf16).astype(f32)
    return jnp.concatenate([high, rows - high], axis=0).astype(bf16)


def force_rows(block, sums):
    products = sums * strength_rows(block)
    half = products[0:8] + products[8:16]
    summed = half[0:4] + half[4:8]
    return block[0:3] * summed[0:1] - summed[1:4]


def kernel(
    n_row, n_col, slots,
    pos_in, strength_in, live_in, send_in, partner_in, parent_block_in, parent_cell_in,
    force, cell_out, top_out,
    pos, strength, live, send_smem, partner_smem, send_vmem, partner_vmem, parent_block, parent_cell, turned, own, coef, charge, sent, received, back, returned, near, highs, lows,
    cell_sent, cell_got, top_sent, top_got, row_sent, row_got,
    sent_sem, received_sem, back_sem, returned_sem, cell_sent_sem, cell_got_sem, top_sent_sem, top_got_sem,
    row_sent_sem, row_got_sem, input_sem,
):
    moves = (
        (live_in, live), (pos_in, pos), (strength_in, strength), (send_in, send_smem), (partner_in, partner_smem),
        (send_in, send_vmem), (partner_in, partner_vmem), (parent_block_in, parent_block), (parent_cell_in, parent_cell),
    )
    inputs = [pltpu.make_async_copy(a, b, input_sem.at[at]) for at, (a, b) in enumerate(moves)]
    for copy in inputs:
        copy.start()
    blocks, width = pos.shape[1], pos.shape[2]
    share = cell_got.shape[1]
    groups = slots // GROUP
    my_row, me = lax.axis_index("row"), lax.axis_index("col")

    my_z, my_y = lax.div(me, RING), lax.rem(me, RING)

    def source(code):
        return lax.rem(my_z + lax.rem(code[0], RING), RING) * RING + lax.rem(my_y + lax.rem(code[1], RING), RING)

    def target(code):
        z = lax.rem(my_z + RING - lax.rem(code[0], RING), RING)
        return z * RING + lax.rem(my_y + RING - lax.rem(code[1], RING), RING)

    def next_code(code):
        return lax.div(code[0], RING), lax.div(code[1], RING)

    barrier = pltpu.get_barrier_semaphore()

    def greet_col(step, carry):
        pl.semaphore_signal(barrier, inc=1, device_id={"col": lax.rem(me + step, n_col)}, device_id_type=MESH)
        return carry

    def greet_row(step, carry):
        pl.semaphore_signal(barrier, inc=1, device_id={"row": lax.rem(my_row + step, n_row)}, device_id_type=MESH)
        return carry

    lax.fori_loop(1, n_col, greet_col, 0)
    lax.fori_loop(1, n_row, greet_row, 0)

    for copy in inputs:
        copy.wait()

    same = row_ids((blocks, blocks)) == lax.broadcasted_iota(i32, (blocks, blocks), 1)
    counts = jnp.sum(jnp.where(same, live[...], 0).astype(f32), axis=1, keepdims=True)
    lane = lax.broadcasted_iota(i32, (blocks, width), 1).astype(f32)
    mask = jnp.where(lane < counts, 1.0, 0.0)
    x = [pos[c] for c in range(3)]
    q = [strength[c] * mask for c in range(3)]
    squares = x[0] * x[0] + x[1] * x[1] + x[2] * x[2]
    for c, rows in enumerate(x + q + [squares, jnp.ones_like(squares)]):
        for part in range(width // 128):
            turned[part, pl.ds(c, blocks, stride=8), :] = rows[:, part * 128 : part * 128 + 128]
    for part in range(width // 128):
        own[:, :, part * 128 : part * 128 + 128] = turned[part].reshape(blocks, 8, 128)

    def own_block(index):
        return own[index]

    def gather_to(buffer, receiver):
        for k in range(slots):
            buffer[receiver, LINES * k : LINES * k + LINES] = own_block(send_smem[receiver, k])[0:LINES]

    gather_to(sent, me)
    stay = pltpu.make_async_copy(sent.at[me], received.at[me], received_sem.at[me])
    stay.start()
    pl.semaphore_wait(barrier, n_col + n_row - 2)

    def send_copy(peer):
        return pltpu.make_async_remote_copy(
            src_ref=sent.at[peer], dst_ref=received.at[me], send_sem=sent_sem.at[peer],
            recv_sem=received_sem.at[me], device_id={"col": peer}, device_id_type=MESH)

    def start_send(peer):
        part = slots * LINES // CHUNKS
        for chunk in range(CHUNKS):
            lines = pl.ds(chunk * part, part)
            pltpu.make_async_remote_copy(
                src_ref=sent.at[peer, lines], dst_ref=received.at[me, lines], send_sem=sent_sem.at[peer],
                recv_sem=received_sem.at[me], device_id={"col": peer}, device_id_type=MESH).start()

    def arrival(peer):
        return pltpu.make_async_remote_copy(
            src_ref=sent.at[peer], dst_ref=received.at[peer], send_sem=sent_sem.at[peer],
            recv_sem=received_sem.at[peer], device_id={"col": peer}, device_id_type=MESH)

    def back_copy(peer):
        return pltpu.make_async_remote_copy(
            src_ref=back.at[peer], dst_ref=returned.at[me], send_sem=back_sem.at[peer],
            recv_sem=returned_sem.at[me], device_id={"col": peer}, device_id_type=MESH)

    def back_arrival(peer):
        return pltpu.make_async_remote_copy(
            src_ref=back.at[peer], dst_ref=returned.at[peer], send_sem=back_sem.at[peer],
            recv_sem=returned_sem.at[peer], device_id={"col": peer}, device_id_type=MESH)

    def cell_copy(peer, at):
        return pltpu.make_async_remote_copy(
            src_ref=cell_sent.at[peer], dst_ref=cell_got.at[at], send_sem=cell_sent_sem.at[peer],
            recv_sem=cell_got_sem.at[at], device_id={"col": peer}, device_id_type=MESH)

    def top_copy(peer, at):
        return pltpu.make_async_remote_copy(
            src_ref=top_sent, dst_ref=top_got.at[at], send_sem=top_sent_sem.at[peer],
            recv_sem=top_got_sem.at[at], device_id={"col": peer}, device_id_type=MESH)

    def row_copy(peer, at):
        return pltpu.make_async_remote_copy(
            src_ref=row_sent, dst_ref=row_got.at[at], send_sem=row_sent_sem.at[peer],
            recv_sem=row_got_sem.at[at], device_id={"row": peer}, device_id_type=MESH)

    def send_step(step, code):
        peer = target(code)
        gather_to(sent, peer)
        start_send(peer)
        return next_code(code)

    codes = (jnp.int32(CODE_Z), jnp.int32(CODE_Y))
    send_code = lax.fori_loop(0, AHEAD, send_step, codes)

    def prepare(step, carry):
        for u in range(PREPARED):
            block = step * PREPARED + u
            tile = own_block(block)
            coef[block] = jnp.transpose(distance_coefficients(tile)).astype(bf16)
            charge[block] = charge_features(tile)
        return carry

    lax.fori_loop(0, blocks // PREPARED, prepare, 0)

    def partner_of(sender, k):
        return jnp.maximum(partner_smem[sender, k], 0)

    def compute_one(buffer, sender, group, slot, u):
        k = group * GROUP + u
        features = distance_features(tile_of(buffer[sender, LINES * k : LINES * k + LINES]))
        squared = dot(coef[partner_of(sender, k)], features, (1, 0))
        inverse = lax.rsqrt(squared)
        cubed = inverse * inverse * inverse
        high = cubed.astype(bf16)
        highs[slot, u] = high
        lows[slot, u] = (cubed - high.astype(f32)).astype(bf16)

    def use_one(buffer, sender, group, slot, u):
        k = group * GROUP + u
        near_at = partner_of(sender, k)
        block = buffer[sender, LINES * k : LINES * k + LINES]
        high, low = highs[slot, u], lows[slot, u]
        own_charge = charge[near_at]
        sums = dot(own_charge, high, (1, 0))
        sums = sums[0:16] + sums[16:32] + dot(own_charge[0:16], low, (1, 0))
        valid = jnp.clip(partner_smem[sender, k] + 1, 0, 1).astype(f32)
        rows = force_rows(block, sums) * valid
        for l in range(3):
            back[sender, l, k : k + 1] = rows[l : l + 1]
        far_charge = charge_features(block)
        sums = dot(far_charge, high, (1, 1))
        sums = sums[0:16] + sums[16:32] + dot(far_charge[0:16], low, (1, 1))
        rows = force_rows(own_block(near_at), sums)
        for l in range(3):
            near[l, sender, k : k + 1] = rows[l : l + 1]

    def advance(later, now, slot):
        for u in range(GROUP):
            if later is not None:
                compute_one(*later, 1 - slot, u)
            if now is not None:
                use_one(*now, slot, u)

    columns = lax.broadcasted_iota(i32, (blocks, 128), 1)
    moments = jnp.zeros((blocks, 128), f32)
    terms = q + [q[c] * x[l] for c in range(3) for l in range(3)]
    for m, term in enumerate(terms):
        moments = jnp.where(columns == m, jnp.sum(term, axis=1, keepdims=True), moments)
    moments = moments * MOMENT_UNIT
    cells = n_col * share
    cell_hot = jnp.where(row_ids((cells, blocks)) == parent_block[...], 1.0, 0.0).astype(bf16)
    cell_part = hot_dot(cell_hot, moments)
    cell_sent[...] = cell_part.reshape(n_col, share, 128)
    cell_got[me] = cell_sent[me]
    top_hot = jnp.where(row_ids((C2, cells)) == parent_cell[...], 1.0, 0.0).astype(bf16)
    top_part = hot_dot(top_hot, cell_part)
    padded = jnp.concatenate([top_part, jnp.zeros((128 - C2, 128), f32)], axis=0)
    top_sent[...] = jnp.transpose(padded)[0:16]
    top_got[me] = top_sent[...]

    def moment_step(step, carry):
        peer = lax.rem(me + n_col - step, n_col)
        cell_copy(peer, me).start()
        top_copy(peer, me).start()
        return carry

    lax.fori_loop(1, n_col, moment_step, 0)

    def sum_of(got, count):
        total = got[0]
        for at in range(1, count):
            total = total + got[at]
        return total

    half = groups // 2
    advance((sent, me, half), None, 1)
    for group in range(half, groups - 1):
        advance((sent, me, group + 1), (sent, me, group), (group - half) % 2)

    first = source(codes)
    arrival(first).wait_recv()
    advance((received, first, 0), (sent, me, groups - 1), 1)

    def sum_tops():
        def wait_moments(step, carry):
            peer = lax.rem(me + step, n_col)
            cell_copy(peer, peer).wait_recv()
            top_copy(peer, peer).wait_recv()
            return carry

        lax.fori_loop(1, n_col, wait_moments, 0)
        row_sent[...] = sum_of(top_got, n_col)
        row_got[my_row] = row_sent[...]

        def row_step(step, carry):
            row_copy(lax.rem(my_row + step, n_row), my_row).start()
            return carry

        lax.fori_loop(1, n_row, row_step, 0)

    def sender_step(step, carry):
        code, send_code = carry[0:2], carry[2:4]
        sender = source(code)
        following_code = next_code(code)
        following = source(following_code)

        @pl.when(step + AHEAD < n_col - 1)
        def _():
            send_step(step, send_code)

        @pl.when(step == n_col // 2)
        def _():
            sum_tops()

        for group in range(groups - 1):
            advance((received, sender, group + 1), (received, sender, group), group % 2)
        arrival(following).wait_recv()
        advance((received, following, 0), (received, sender, groups - 1), (groups - 1) % 2)
        back_copy(sender).start()
        return following_code + next_code(send_code)

    lax.fori_loop(0, n_col - 1, sender_step, codes + send_code)

    for group in range(half):
        later = (received, me, group + 1) if group + 1 < half else None
        advance(later, (received, me, group), group % 2)
    cell_sum = sum_of(cell_got, n_col)
    cell_rows = jnp.concatenate([cell_sum, jnp.zeros((128 - share, 128), f32)], axis=0)
    cell_out[...] = jnp.transpose(cell_rows)[0:12, 0:share]

    returned[me] = back[me]

    def row_wait(other, carry):
        peer = lax.rem(my_row + other, n_row)
        row_copy(peer, peer).wait_recv()
        return carry

    lax.fori_loop(1, n_row, row_wait, 0)
    top_out[...] = sum_of(row_got, n_row)[0:12, 0:C2]

    pairs = n_col * slots
    pair = lax.broadcasted_iota(i32, (slots, pairs), 1)
    pair_row = row_ids((slots, pairs))
    in_slot = jnp.where(lax.rem(pair, slots) == pair_row, 1.0, 0.0).astype(bf16)
    pair_c = lax.broadcasted_iota(i32, (n_col, pairs), 1)
    in_peer = jnp.where(lax.div(pair_c, slots) == row_ids((n_col, pairs)), 1.0, 0.0)
    block_id = row_ids((blocks, pairs)).astype(f32)

    def hot_of(listed):
        spread = dot(listed[...].astype(f32).astype(bf16), in_slot, (1, 0))
        flat = jnp.sum(spread * in_peer, axis=0, keepdims=True)
        return jnp.where(block_id == flat, 1.0, 0.0).astype(bf16)

    near_hot = hot_of(partner_vmem)
    totals = [hot_dot(near_hot, near[l].reshape(pairs, width)) for l in range(3)]
    sent_hot = hot_of(send_vmem)

    def finish(step, carry):
        peer = lax.rem(me + step, n_col)
        back_arrival(peer).wait_recv()
        return carry

    lax.fori_loop(1, n_col, finish, 0)
    for l in range(3):
        force[l] = totals[l] + hot_dot(sent_hot, returned[:, l].reshape(pairs, width))

    def drain(step, carry):
        peer = lax.rem(me + step, n_col)
        send_copy(peer).wait_send()
        back_copy(peer).wait_send()
        cell_copy(peer, me).wait_send()
        top_copy(peer, me).wait_send()
        return carry

    lax.fori_loop(1, n_col, drain, 0)

    def drain_row(step, carry):
        row_copy(lax.rem(my_row + step, n_row), my_row).wait_send()
        return carry

    lax.fori_loop(1, n_row, drain_row, 0)


def body(positions, strengths, live_count, send_list, partner, parent_block, parent_cell):
    n_row, n_col = lax.axis_size("row"), lax.axis_size("col")
    blocks, width = positions.shape[2:]
    slots = send_list.shape[3]
    cells = parent_cell.shape[1]
    share = cells // n_col
    vmem = pl.BlockSpec(memory_space=pltpu.VMEM)
    hbm = pl.BlockSpec(memory_space=pltpu.HBM)
    dma = pltpu.SemaphoreType.DMA
    force, cell, top = pl.pallas_call(
        functools.partial(kernel, n_row, n_col, slots),
        out_shape=(
            jax.ShapeDtypeStruct((3, blocks, width), f32),
            jax.ShapeDtypeStruct((12, share), f32),
            jax.ShapeDtypeStruct((12, C2), f32),
        ),
        in_specs=[hbm] * 7,
        out_specs=(vmem, vmem, vmem),
        scratch_shapes=[
            pltpu.VMEM((3, blocks, width), f32),
            pltpu.VMEM((3, blocks, width), f32),
            pltpu.VMEM((1, blocks), i32),
            pltpu.SMEM((n_col, slots), i32),
            pltpu.SMEM((n_col, slots), i32),
            pltpu.VMEM((n_col, slots), i32),
            pltpu.VMEM((n_col, slots), i32),
            pltpu.VMEM((1, blocks), i32),
            pltpu.VMEM((1, cells), i32),
            pltpu.VMEM((width // 128, blocks * 8, 128), f32),
            pltpu.VMEM((blocks, 8, width), f32),
            pltpu.VMEM((blocks, width, 48), bf16),
            pltpu.VMEM((blocks, 32, width), bf16),
            pltpu.VMEM((n_col, slots * LINES, width), f32),
            pltpu.VMEM((n_col, slots * LINES, width), f32),
            pltpu.VMEM((n_col, 3, slots, width), f32),
            pltpu.VMEM((n_col, 3, slots, width), f32),
            pltpu.VMEM((3, n_col, slots, width), f32),
            pltpu.VMEM((2, GROUP, width, width), bf16),
            pltpu.VMEM((2, GROUP, width, width), bf16),
            pltpu.VMEM((n_col, share, 128), f32),
            pltpu.VMEM((n_col, share, 128), f32),
            pltpu.VMEM((16, 128), f32),
            pltpu.VMEM((n_col, 16, 128), f32),
            pltpu.VMEM((16, 128), f32),
            pltpu.VMEM((n_row, 16, 128), f32),
            *[dma((n_col,)) for _ in range(8)],
            dma((n_row,)),
            dma((n_row,)),
            dma((9,)),
        ],
        compiler_params=pltpu.CompilerParams(
            collective_id=0, has_side_effects=True, vmem_limit_bytes=40 * 1024 * 1024
        ),
        name="pair_forces",
    )(*[
        pltpu.with_memory_space_constraint(each, pltpu.HBM)
        for each in (
            positions[:, 0], strengths[:, 0], live_count, send_list[0, 0], partner[0, 0], parent_block, parent_cell
        )
    ])
    return force[:, None], cell[:, None, :], top


def solution(mesh):
    placed = (
        P(None, "row", "col", None),
        P(None, "row", "col", None),
        P("row", "col"),
        P("row", "col", None, None),
        P("row", "col", None, None),
        P("row", "col"),
        P("row", None),
    )
    return jax.shard_map(
        body,
        mesh=mesh,
        in_specs=placed,
        out_specs=(P(None, "row", "col", None), P(None, "row", "col"), P()),
        check_vma=False,
    )
```

```python
import functools

import jax
import jax.numpy as jnp
from jax import lax
from jax.experimental import pallas as pl
from jax.experimental.pallas import tpu as pltpu
from jax.sharding import PartitionSpec as P

C2 = 64
CORE_SQUARED = 1.0
MOMENT_UNIT = 0.0625
GROUP = 4
AHEAD = 6
LINES = 6
CHUNKS = 1
PREPARED = 8
RING = 4
OFFSETS = (
    (0, 1), (0, 3), (1, 0), (3, 0), (1, 1), (3, 3), (1, 3), (3, 1),
    (0, 2), (2, 0), (2, 1), (2, 3), (1, 2), (3, 2), (2, 2),
)
CODE_Z = sum(offset[0] * RING**step for step, offset in enumerate(OFFSETS))
CODE_Y = sum(offset[1] * RING**step for step, offset in enumerate(OFFSETS))
f32, bf16, i32 = jnp.float32, jnp.bfloat16, jnp.int32
MESH = pl.DeviceIdType.MESH


def split3(values):
    high = values.astype(bf16).astype(f32)
    rest = values - high
    middle = rest.astype(bf16).astype(f32)
    return high, middle, rest - middle


def dot(left, right, contract):
    return lax.dot_general(left, right, ((contract[0:1], contract[1:2]), ((), ())), preferred_element_type=f32)


def hot_dot(hot, values, contract=(1, 0)):
    high, middle, low = split3(values)
    return (
        dot(hot, high.astype(bf16), contract)
        + dot(hot, middle.astype(bf16), contract)
        + dot(hot, low.astype(bf16), contract)
    )


def row_ids(shape):
    return lax.broadcasted_iota(i32, shape, 0)


def tile_of(block):
    squares = block[0:1] * block[0:1] + block[1:2] * block[1:2] + block[2:3] * block[2:3]
    return jnp.concatenate([block[0:6], squares, jnp.ones_like(squares)], axis=0)


def distance_features(tile):
    high, middle, low = split3(tile)
    return jnp.concatenate([high, high, high, middle, middle, low], axis=0).astype(bf16)


def distance_coefficients(tile):
    row = row_ids(tile.shape)
    squares = tile[6:7] + CORE_SQUARED
    base = jnp.where(row < 3, -2.0 * tile, jnp.where(row == 7, squares, 0.0))
    high, middle, low = split3(base)
    unit = jnp.where(row == 6, 1.0, 0.0)
    first = jnp.where(row < 3, high, unit)
    second = jnp.where(row < 3, middle, 0.0)
    return jnp.concatenate([high + unit, middle, low, first, second, first], axis=0)


def strength_rows(block):
    width = block.shape[1]
    fours = [jnp.broadcast_to(block[c : c + 1], (4, width)) for c in (3, 4, 5)]
    return jnp.concatenate(fours + [jnp.zeros((4, width), f32)], axis=0)


def charge_features(block):
    one = jnp.ones((1, block.shape[1]), f32)
    four = [one, block[0:3]]
    rows = jnp.concatenate(four * 4, axis=0) * strength_rows(block)
    high = rows.astype(bf16).astype(f32)
    return jnp.concatenate([high, rows - high], axis=0).astype(bf16)


def force_rows(block, sums):
    products = sums * strength_rows(block)
    half = products[0:8] + products[8:16]
    summed = half[0:4] + half[4:8]
    return block[0:3] * summed[0:1] - summed[1:4]


def kernel(
    n_row, n_col, slots,
    pos_in, strength_in, live_in, send_in, partner_in, parent_block_in, parent_cell_in,
    force, cell_out, top_out,
    pos, strength, live, send_smem, partner_smem, send_vmem, partner_vmem, parent_block, parent_cell, turned, own, coef, charge, sent, received, back, returned, near, highs, lows, highs_turned, lows_turned,
    cell_sent, cell_got, top_sent, top_got, row_sent, row_got,
    sent_sem, received_sem, back_sem, returned_sem, cell_sent_sem, cell_got_sem, top_sent_sem, top_got_sem,
    row_sent_sem, row_got_sem, input_sem,
):
    moves = (
        (live_in, live), (pos_in, pos), (strength_in, strength), (send_in, send_smem), (partner_in, partner_smem),
        (send_in, send_vmem), (partner_in, partner_vmem), (parent_block_in, parent_block), (parent_cell_in, parent_cell),
    )
    inputs = [pltpu.make_async_copy(a, b, input_sem.at[at]) for at, (a, b) in enumerate(moves)]
    for copy in inputs:
        copy.start()
    blocks, width = pos.shape[1], pos.shape[2]
    share = cell_got.shape[1]
    groups = slots // GROUP
    my_row, me = lax.axis_index("row"), lax.axis_index("col")

    my_z, my_y = lax.div(me, RING), lax.rem(me, RING)

    def source(code):
        return lax.rem(my_z + lax.rem(code[0], RING), RING) * RING + lax.rem(my_y + lax.rem(code[1], RING), RING)

    def target(code):
        z = lax.rem(my_z + RING - lax.rem(code[0], RING), RING)
        return z * RING + lax.rem(my_y + RING - lax.rem(code[1], RING), RING)

    def next_code(code):
        return lax.div(code[0], RING), lax.div(code[1], RING)

    barrier = pltpu.get_barrier_semaphore()

    def greet_col(step, carry):
        pl.semaphore_signal(barrier, inc=1, device_id={"col": lax.rem(me + step, n_col)}, device_id_type=MESH)
        return carry

    def greet_row(step, carry):
        pl.semaphore_signal(barrier, inc=1, device_id={"row": lax.rem(my_row + step, n_row)}, device_id_type=MESH)
        return carry

    lax.fori_loop(1, n_col, greet_col, 0)
    lax.fori_loop(1, n_row, greet_row, 0)

    for copy in inputs:
        copy.wait()

    same = row_ids((blocks, blocks)) == lax.broadcasted_iota(i32, (blocks, blocks), 1)
    counts = jnp.sum(jnp.where(same, live[...], 0).astype(f32), axis=1, keepdims=True)
    lane = lax.broadcasted_iota(i32, (blocks, width), 1).astype(f32)
    mask = jnp.where(lane < counts, 1.0, 0.0)
    x = [pos[c] for c in range(3)]
    q = [strength[c] * mask for c in range(3)]
    squares = x[0] * x[0] + x[1] * x[1] + x[2] * x[2]
    for c, rows in enumerate(x + q + [squares, jnp.ones_like(squares)]):
        for part in range(width // 128):
            turned[part, pl.ds(c, blocks, stride=8), :] = rows[:, part * 128 : part * 128 + 128]
    for part in range(width // 128):
        own[:, :, part * 128 : part * 128 + 128] = turned[part].reshape(blocks, 8, 128)

    def own_block(index):
        return own[index]

    def gather_to(buffer, receiver):
        for k in range(slots):
            buffer[receiver, LINES * k : LINES * k + LINES] = own_block(send_smem[receiver, k])[0:LINES]

    gather_to(sent, me)
    stay = pltpu.make_async_copy(sent.at[me], received.at[me], received_sem.at[me])
    stay.start()
    pl.semaphore_wait(barrier, n_col + n_row - 2)

    def send_copy(peer):
        return pltpu.make_async_remote_copy(
            src_ref=sent.at[peer], dst_ref=received.at[me], send_sem=sent_sem.at[peer],
            recv_sem=received_sem.at[me], device_id={"col": peer}, device_id_type=MESH)

    def start_send(peer):
        part = slots * LINES // CHUNKS
        for chunk in range(CHUNKS):
            lines = pl.ds(chunk * part, part)
            pltpu.make_async_remote_copy(
                src_ref=sent.at[peer, lines], dst_ref=received.at[me, lines], send_sem=sent_sem.at[peer],
                recv_sem=received_sem.at[me], device_id={"col": peer}, device_id_type=MESH).start()

    def arrival(peer):
        return pltpu.make_async_remote_copy(
            src_ref=sent.at[peer], dst_ref=received.at[peer], send_sem=sent_sem.at[peer],
            recv_sem=received_sem.at[peer], device_id={"col": peer}, device_id_type=MESH)

    def back_copy(peer):
        return pltpu.make_async_remote_copy(
            src_ref=back.at[peer], dst_ref=returned.at[me], send_sem=back_sem.at[peer],
            recv_sem=returned_sem.at[me], device_id={"col": peer}, device_id_type=MESH)

    def back_arrival(peer):
        return pltpu.make_async_remote_copy(
            src_ref=back.at[peer], dst_ref=returned.at[peer], send_sem=back_sem.at[peer],
            recv_sem=returned_sem.at[peer], device_id={"col": peer}, device_id_type=MESH)

    def cell_copy(peer, at):
        return pltpu.make_async_remote_copy(
            src_ref=cell_sent.at[peer], dst_ref=cell_got.at[at], send_sem=cell_sent_sem.at[peer],
            recv_sem=cell_got_sem.at[at], device_id={"col": peer}, device_id_type=MESH)

    def top_copy(peer, at):
        return pltpu.make_async_remote_copy(
            src_ref=top_sent, dst_ref=top_got.at[at], send_sem=top_sent_sem.at[peer],
            recv_sem=top_got_sem.at[at], device_id={"col": peer}, device_id_type=MESH)

    def row_copy(peer, at):
        return pltpu.make_async_remote_copy(
            src_ref=row_sent, dst_ref=row_got.at[at], send_sem=row_sent_sem.at[peer],
            recv_sem=row_got_sem.at[at], device_id={"row": peer}, device_id_type=MESH)

    def send_step(step, code):
        peer = target(code)
        gather_to(sent, peer)
        start_send(peer)
        return next_code(code)

    codes = (jnp.int32(CODE_Z), jnp.int32(CODE_Y))
    send_code = lax.fori_loop(0, AHEAD, send_step, codes)

    def prepare(step, carry):
        for u in range(PREPARED):
            block = step * PREPARED + u
            tile = own_block(block)
            coef[block] = jnp.transpose(distance_coefficients(tile)).astype(bf16)
            charge[block] = charge_features(tile)
        return carry

    lax.fori_loop(0, blocks // PREPARED, prepare, 0)

    def partner_of(sender, k):
        return jnp.maximum(partner_smem[sender, k], 0)

    def compute_one(buffer, sender, group, slot, u):
        k = group * GROUP + u
        features = distance_features(tile_of(buffer[sender, LINES * k : LINES * k + LINES]))
        squared = dot(coef[partner_of(sender, k)], features, (1, 0))
        inverse = lax.rsqrt(squared)
        cubed = inverse * inverse * inverse
        high = cubed.astype(bf16)
        low = (cubed - high.astype(f32)).astype(bf16)
        highs[slot, u] = high
        lows[slot, u] = low
        highs_turned[slot, u] = jnp.transpose(high)
        lows_turned[slot, u] = jnp.transpose(low)

    def use_one(buffer, sender, group, slot, u):
        k = group * GROUP + u
        near_at = partner_of(sender, k)
        block = buffer[sender, LINES * k : LINES * k + LINES]
        high, low = highs[slot, u], lows[slot, u]
        own_charge = charge[near_at]
        sums = dot(own_charge, high, (1, 0))
        sums = sums[0:16] + sums[16:32] + dot(own_charge[0:16], low, (1, 0))
        valid = jnp.clip(partner_smem[sender, k] + 1, 0, 1).astype(f32)
        rows = force_rows(block, sums) * valid
        for l in range(3):
            back[sender, l, k : k + 1] = rows[l : l + 1]
        far_charge = charge_features(block)
        sums = dot(far_charge, highs_turned[slot, u], (1, 0))
        sums = sums[0:16] + sums[16:32] + dot(far_charge[0:16], lows_turned[slot, u], (1, 0))
        rows = force_rows(own_block(near_at), sums)
        for l in range(3):
            near[l, sender, k : k + 1] = rows[l : l + 1]

    def advance(later, now, slot):
        for u in range(GROUP):
            if later is not None:
                compute_one(*later, 1 - slot, u)
            if now is not None:
                use_one(*now, slot, u)

    columns = lax.broadcasted_iota(i32, (blocks, 128), 1)
    moments = jnp.zeros((blocks, 128), f32)
    terms = q + [q[c] * x[l] for c in range(3) for l in range(3)]
    for m, term in enumerate(terms):
        moments = jnp.where(columns == m, jnp.sum(term, axis=1, keepdims=True), moments)
    moments = moments * MOMENT_UNIT
    cells = n_col * share
    cell_hot = jnp.where(row_ids((cells, blocks)) == parent_block[...], 1.0, 0.0).astype(bf16)
    cell_part = hot_dot(cell_hot, moments)
    cell_sent[...] = cell_part.reshape(n_col, share, 128)
    cell_got[me] = cell_sent[me]
    top_hot = jnp.where(row_ids((C2, cells)) == parent_cell[...], 1.0, 0.0).astype(bf16)
    top_part = hot_dot(top_hot, cell_part)
    padded = jnp.concatenate([top_part, jnp.zeros((128 - C2, 128), f32)], axis=0)
    top_sent[...] = jnp.transpose(padded)[0:16]
    top_got[me] = top_sent[...]

    def moment_step(step, carry):
        peer = lax.rem(me + n_col - step, n_col)
        cell_copy(peer, me).start()
        top_copy(peer, me).start()
        return carry

    lax.fori_loop(1, n_col, moment_step, 0)

    def sum_of(got, count):
        total = got[0]
        for at in range(1, count):
            total = total + got[at]
        return total

    half = groups // 2
    advance((sent, me, half), None, 1)
    for group in range(half, groups - 1):
        advance((sent, me, group + 1), (sent, me, group), (group - half) % 2)

    first = source(codes)
    arrival(first).wait_recv()
    advance((received, first, 0), (sent, me, groups - 1), 1)

    def sum_tops():
        def wait_moments(step, carry):
            peer = lax.rem(me + step, n_col)
            cell_copy(peer, peer).wait_recv()
            top_copy(peer, peer).wait_recv()
            return carry

        lax.fori_loop(1, n_col, wait_moments, 0)
        row_sent[...] = sum_of(top_got, n_col)
        row_got[my_row] = row_sent[...]

        def row_step(step, carry):
            row_copy(lax.rem(my_row + step, n_row), my_row).start()
            return carry

        lax.fori_loop(1, n_row, row_step, 0)

    def sender_step(step, carry):
        code, send_code = carry[0:2], carry[2:4]
        sender = source(code)
        following_code = next_code(code)
        following = source(following_code)

        @pl.when(step + AHEAD < n_col - 1)
        def _():
            send_step(step, send_code)

        @pl.when(step == n_col // 2)
        def _():
            sum_tops()

        for group in range(groups - 1):
            advance((received, sender, group + 1), (received, sender, group), group % 2)
        arrival(following).wait_recv()
        advance((received, following, 0), (received, sender, groups - 1), (groups - 1) % 2)
        back_copy(sender).start()
        return following_code + next_code(send_code)

    lax.fori_loop(0, n_col - 1, sender_step, codes + send_code)

    for group in range(half):
        later = (received, me, group + 1) if group + 1 < half else None
        advance(later, (received, me, group), group % 2)
    cell_sum = sum_of(cell_got, n_col)
    cell_rows = jnp.concatenate([cell_sum, jnp.zeros((128 - share, 128), f32)], axis=0)
    cell_out[...] = jnp.transpose(cell_rows)[0:12, 0:share]

    returned[me] = back[me]

    def row_wait(other, carry):
        peer = lax.rem(my_row + other, n_row)
        row_copy(peer, peer).wait_recv()
        return carry

    lax.fori_loop(1, n_row, row_wait, 0)
    top_out[...] = sum_of(row_got, n_row)[0:12, 0:C2]

    pairs = n_col * slots
    pair = lax.broadcasted_iota(i32, (slots, pairs), 1)
    pair_row = row_ids((slots, pairs))
    in_slot = jnp.where(lax.rem(pair, slots) == pair_row, 1.0, 0.0).astype(bf16)
    pair_c = lax.broadcasted_iota(i32, (n_col, pairs), 1)
    in_peer = jnp.where(lax.div(pair_c, slots) == row_ids((n_col, pairs)), 1.0, 0.0)
    block_id = row_ids((blocks, pairs)).astype(f32)

    def hot_of(listed):
        spread = dot(listed[...].astype(f32).astype(bf16), in_slot, (1, 0))
        flat = jnp.sum(spread * in_peer, axis=0, keepdims=True)
        return jnp.where(block_id == flat, 1.0, 0.0).astype(bf16)

    near_hot = hot_of(partner_vmem)
    totals = [hot_dot(near_hot, near[l].reshape(pairs, width)) for l in range(3)]
    sent_hot = hot_of(send_vmem)

    def finish(step, carry):
        peer = lax.rem(me + step, n_col)
        back_arrival(peer).wait_recv()
        return carry

    lax.fori_loop(1, n_col, finish, 0)
    for l in range(3):
        force[l] = totals[l] + hot_dot(sent_hot, returned[:, l].reshape(pairs, width))

    def drain(step, carry):
        peer = lax.rem(me + step, n_col)
        send_copy(peer).wait_send()
        back_copy(peer).wait_send()
        cell_copy(peer, me).wait_send()
        top_copy(peer, me).wait_send()
        return carry

    lax.fori_loop(1, n_col, drain, 0)

    def drain_row(step, carry):
        row_copy(lax.rem(my_row + step, n_row), my_row).wait_send()
        return carry

    lax.fori_loop(1, n_row, drain_row, 0)


def body(positions, strengths, live_count, send_list, partner, parent_block, parent_cell):
    n_row, n_col = lax.axis_size("row"), lax.axis_size("col")
    blocks, width = positions.shape[2:]
    slots = send_list.shape[3]
    cells = parent_cell.shape[1]
    share = cells // n_col
    vmem = pl.BlockSpec(memory_space=pltpu.VMEM)
    hbm = pl.BlockSpec(memory_space=pltpu.HBM)
    dma = pltpu.SemaphoreType.DMA
    force, cell, top = pl.pallas_call(
        functools.partial(kernel, n_row, n_col, slots),
        out_shape=(
            jax.ShapeDtypeStruct((3, blocks, width), f32),
            jax.ShapeDtypeStruct((12, share), f32),
            jax.ShapeDtypeStruct((12, C2), f32),
        ),
        in_specs=[hbm] * 7,
        out_specs=(vmem, vmem, vmem),
        scratch_shapes=[
            pltpu.VMEM((3, blocks, width), f32),
            pltpu.VMEM((3, blocks, width), f32),
            pltpu.VMEM((1, blocks), i32),
            pltpu.SMEM((n_col, slots), i32),
            pltpu.SMEM((n_col, slots), i32),
            pltpu.VMEM((n_col, slots), i32),
            pltpu.VMEM((n_col, slots), i32),
            pltpu.VMEM((1, blocks), i32),
            pltpu.VMEM((1, cells), i32),
            pltpu.VMEM((width // 128, blocks * 8, 128), f32),
            pltpu.VMEM((blocks, 8, width), f32),
            pltpu.VMEM((blocks, width, 48), bf16),
            pltpu.VMEM((blocks, 32, width), bf16),
            pltpu.VMEM((n_col, slots * LINES, width), f32),
            pltpu.VMEM((n_col, slots * LINES, width), f32),
            pltpu.VMEM((n_col, 3, slots, width), f32),
            pltpu.VMEM((n_col, 3, slots, width), f32),
            pltpu.VMEM((3, n_col, slots, width), f32),
            pltpu.VMEM((2, GROUP, width, width), bf16),
            pltpu.VMEM((2, GROUP, width, width), bf16),
            pltpu.VMEM((2, GROUP, width, width), bf16),
            pltpu.VMEM((2, GROUP, width, width), bf16),
            pltpu.VMEM((n_col, share, 128), f32),
            pltpu.VMEM((n_col, share, 128), f32),
            pltpu.VMEM((16, 128), f32),
            pltpu.VMEM((n_col, 16, 128), f32),
            pltpu.VMEM((16, 128), f32),
            pltpu.VMEM((n_row, 16, 128), f32),
            *[dma((n_col,)) for _ in range(8)],
            dma((n_row,)),
            dma((n_row,)),
            dma((9,)),
        ],
        compiler_params=pltpu.CompilerParams(
            collective_id=0, has_side_effects=True, vmem_limit_bytes=40 * 1024 * 1024
        ),
        name="pair_forces",
    )(*[
        pltpu.with_memory_space_constraint(each, pltpu.HBM)
        for each in (
            positions[:, 0], strengths[:, 0], live_count, send_list[0, 0], partner[0, 0], parent_block, parent_cell
        )
    ])
    return force[:, None], cell[:, None, :], top


def solution(mesh):
    placed = (
        P(None, "row", "col", None),
        P(None, "row", "col", None),
        P("row", "col"),
        P("row", "col", None, None),
        P("row", "col", None, None),
        P("row", "col"),
        P("row", None),
    )
    return jax.shard_map(
        body,
        mesh=mesh,
        in_specs=placed,
        out_specs=(P(None, "row", "col", None), P(None, "row", "col"), P()),
        check_vma=False,
    )
```

```python
import functools

import jax
import jax.numpy as jnp
from jax import lax
from jax.experimental import pallas as pl
from jax.experimental.pallas import tpu as pltpu
from jax.sharding import PartitionSpec as P

C2 = 64
CORE_SQUARED = 1.0
MOMENT_UNIT = 0.0625
GROUP = 8
AHEAD = 6
LINES = 6
CHUNKS = 1
PREPARED = 8
RING = 4
OFFSETS = (
    (0, 1), (0, 3), (1, 0), (3, 0), (1, 1), (3, 3), (1, 3), (3, 1),
    (0, 2), (2, 0), (2, 1), (2, 3), (1, 2), (3, 2), (2, 2),
)
CODE_Z = sum(offset[0] * RING**step for step, offset in enumerate(OFFSETS))
CODE_Y = sum(offset[1] * RING**step for step, offset in enumerate(OFFSETS))
f32, bf16, i32 = jnp.float32, jnp.bfloat16, jnp.int32
MESH = pl.DeviceIdType.MESH


def split3(values):
    high = values.astype(bf16).astype(f32)
    rest = values - high
    middle = rest.astype(bf16).astype(f32)
    return high, middle, rest - middle


def dot(left, right, contract):
    return lax.dot_general(left, right, ((contract[0:1], contract[1:2]), ((), ())), preferred_element_type=f32)


def hot_dot(hot, values, contract=(1, 0)):
    high, middle, low = split3(values)
    return (
        dot(hot, high.astype(bf16), contract)
        + dot(hot, middle.astype(bf16), contract)
        + dot(hot, low.astype(bf16), contract)
    )


def row_ids(shape):
    return lax.broadcasted_iota(i32, shape, 0)


def tile_of(block):
    squares = block[0:1] * block[0:1] + block[1:2] * block[1:2] + block[2:3] * block[2:3]
    return jnp.concatenate([block[0:6], squares, jnp.ones_like(squares)], axis=0)


def distance_features(tile):
    high, middle, low = split3(tile)
    return jnp.concatenate([high, high, high, middle, middle, low], axis=0).astype(bf16)


def distance_coefficients(tile):
    row = row_ids(tile.shape)
    squares = tile[6:7] + CORE_SQUARED
    base = jnp.where(row < 3, -2.0 * tile, jnp.where(row == 7, squares, 0.0))
    high, middle, low = split3(base)
    unit = jnp.where(row == 6, 1.0, 0.0)
    first = jnp.where(row < 3, high, unit)
    second = jnp.where(row < 3, middle, 0.0)
    return jnp.concatenate([high + unit, middle, low, first, second, first], axis=0)


def strength_rows(block):
    width = block.shape[1]
    fours = [jnp.broadcast_to(block[c : c + 1], (4, width)) for c in (3, 4, 5)]
    return jnp.concatenate(fours + [jnp.zeros((4, width), f32)], axis=0)


def charge_features(block):
    one = jnp.ones((1, block.shape[1]), f32)
    four = [one, block[0:3]]
    rows = jnp.concatenate(four * 4, axis=0) * strength_rows(block)
    high = rows.astype(bf16).astype(f32)
    return jnp.concatenate([high, rows - high], axis=0).astype(bf16)


def force_rows(block, sums):
    products = sums * strength_rows(block)
    half = products[0:8] + products[8:16]
    summed = half[0:4] + half[4:8]
    return block[0:3] * summed[0:1] - summed[1:4]


def kernel(
    n_row, n_col, slots,
    pos_in, strength_in, live_in, send_in, partner_in, parent_block_in, parent_cell_in,
    force, cell_out, top_out,
    pos, strength, live, send_smem, partner_smem, send_vmem, partner_vmem, parent_block, parent_cell, turned, own, coef, charge, sent, received, back, returned, near, highs, lows, highs_turned, lows_turned,
    cell_sent, cell_got, top_sent, top_got, row_sent, row_got,
    sent_sem, received_sem, back_sem, returned_sem, cell_sent_sem, cell_got_sem, top_sent_sem, top_got_sem,
    row_sent_sem, row_got_sem, input_sem,
):
    moves = (
        (live_in, live), (pos_in, pos), (strength_in, strength), (send_in, send_smem), (partner_in, partner_smem),
        (send_in, send_vmem), (partner_in, partner_vmem), (parent_block_in, parent_block), (parent_cell_in, parent_cell),
    )
    inputs = [pltpu.make_async_copy(a, b, input_sem.at[at]) for at, (a, b) in enumerate(moves)]
    for copy in inputs:
        copy.start()
    blocks, width = pos.shape[1], pos.shape[2]
    share = cell_got.shape[1]
    groups = slots // GROUP
    my_row, me = lax.axis_index("row"), lax.axis_index("col")

    my_z, my_y = lax.div(me, RING), lax.rem(me, RING)

    def source(code):
        return lax.rem(my_z + lax.rem(code[0], RING), RING) * RING + lax.rem(my_y + lax.rem(code[1], RING), RING)

    def target(code):
        z = lax.rem(my_z + RING - lax.rem(code[0], RING), RING)
        return z * RING + lax.rem(my_y + RING - lax.rem(code[1], RING), RING)

    def next_code(code):
        return lax.div(code[0], RING), lax.div(code[1], RING)

    barrier = pltpu.get_barrier_semaphore()

    def greet_col(step, carry):
        pl.semaphore_signal(barrier, inc=1, device_id={"col": lax.rem(me + step, n_col)}, device_id_type=MESH)
        return carry

    def greet_row(step, carry):
        pl.semaphore_signal(barrier, inc=1, device_id={"row": lax.rem(my_row + step, n_row)}, device_id_type=MESH)
        return carry

    lax.fori_loop(1, n_col, greet_col, 0)
    lax.fori_loop(1, n_row, greet_row, 0)

    for copy in inputs:
        copy.wait()

    same = row_ids((blocks, blocks)) == lax.broadcasted_iota(i32, (blocks, blocks), 1)
    counts = jnp.sum(jnp.where(same, live[...], 0).astype(f32), axis=1, keepdims=True)
    lane = lax.broadcasted_iota(i32, (blocks, width), 1).astype(f32)
    mask = jnp.where(lane < counts, 1.0, 0.0)
    x = [pos[c] for c in range(3)]
    q = [strength[c] * mask for c in range(3)]
    squares = x[0] * x[0] + x[1] * x[1] + x[2] * x[2]
    for c, rows in enumerate(x + q + [squares, jnp.ones_like(squares)]):
        for part in range(width // 128):
            turned[part, pl.ds(c, blocks, stride=8), :] = rows[:, part * 128 : part * 128 + 128]
    for part in range(width // 128):
        own[:, :, part * 128 : part * 128 + 128] = turned[part].reshape(blocks, 8, 128)

    def own_block(index):
        return own[index]

    def gather_to(buffer, receiver):
        for k in range(slots):
            buffer[receiver, LINES * k : LINES * k + LINES] = own_block(send_smem[receiver, k])[0:LINES]

    gather_to(sent, me)
    stay = pltpu.make_async_copy(sent.at[me], received.at[me], received_sem.at[me])
    stay.start()
    pl.semaphore_wait(barrier, n_col + n_row - 2)

    def send_copy(peer):
        return pltpu.make_async_remote_copy(
            src_ref=sent.at[peer], dst_ref=received.at[me], send_sem=sent_sem.at[peer],
            recv_sem=received_sem.at[me], device_id={"col": peer}, device_id_type=MESH)

    def start_send(peer):
        part = slots * LINES // CHUNKS
        for chunk in range(CHUNKS):
            lines = pl.ds(chunk * part, part)
            pltpu.make_async_remote_copy(
                src_ref=sent.at[peer, lines], dst_ref=received.at[me, lines], send_sem=sent_sem.at[peer],
                recv_sem=received_sem.at[me], device_id={"col": peer}, device_id_type=MESH).start()

    def arrival(peer):
        return pltpu.make_async_remote_copy(
            src_ref=sent.at[peer], dst_ref=received.at[peer], send_sem=sent_sem.at[peer],
            recv_sem=received_sem.at[peer], device_id={"col": peer}, device_id_type=MESH)

    def back_copy(peer):
        return pltpu.make_async_remote_copy(
            src_ref=back.at[peer], dst_ref=returned.at[me], send_sem=back_sem.at[peer],
            recv_sem=returned_sem.at[me], device_id={"col": peer}, device_id_type=MESH)

    def start_back(peer, group):
        lines = slice(group * GROUP, group * GROUP + GROUP)
        pltpu.make_async_remote_copy(
            src_ref=back.at[peer, :, lines], dst_ref=returned.at[me, :, lines], send_sem=back_sem.at[peer],
            recv_sem=returned_sem.at[me], device_id={"col": peer}, device_id_type=MESH).start()

    def back_arrival(peer):
        return pltpu.make_async_remote_copy(
            src_ref=back.at[peer], dst_ref=returned.at[peer], send_sem=back_sem.at[peer],
            recv_sem=returned_sem.at[peer], device_id={"col": peer}, device_id_type=MESH)

    def cell_copy(peer, at):
        return pltpu.make_async_remote_copy(
            src_ref=cell_sent.at[peer], dst_ref=cell_got.at[at], send_sem=cell_sent_sem.at[peer],
            recv_sem=cell_got_sem.at[at], device_id={"col": peer}, device_id_type=MESH)

    def top_copy(peer, at):
        return pltpu.make_async_remote_copy(
            src_ref=top_sent, dst_ref=top_got.at[at], send_sem=top_sent_sem.at[peer],
            recv_sem=top_got_sem.at[at], device_id={"col": peer}, device_id_type=MESH)

    def row_copy(peer, at):
        return pltpu.make_async_remote_copy(
            src_ref=row_sent, dst_ref=row_got.at[at], send_sem=row_sent_sem.at[peer],
            recv_sem=row_got_sem.at[at], device_id={"row": peer}, device_id_type=MESH)

    def send_step(step, code):
        peer = target(code)
        gather_to(sent, peer)
        start_send(peer)
        return next_code(code)

    codes = (jnp.int32(CODE_Z), jnp.int32(CODE_Y))
    send_code = lax.fori_loop(0, AHEAD, send_step, codes)

    def prepare(step, carry):
        for u in range(PREPARED):
            block = step * PREPARED + u
            tile = own_block(block)
            coef[block] = jnp.transpose(distance_coefficients(tile)).astype(bf16)
            charge[block] = charge_features(tile)
        return carry

    lax.fori_loop(0, blocks // PREPARED, prepare, 0)

    def partner_of(sender, k):
        return jnp.maximum(partner_smem[sender, k], 0)

    def compute_one(buffer, sender, group, slot, u):
        k = group * GROUP + u
        features = distance_features(tile_of(buffer[sender, LINES * k : LINES * k + LINES]))
        squared = dot(coef[partner_of(sender, k)], features, (1, 0))
        inverse = lax.rsqrt(squared)
        cubed = inverse * inverse * inverse
        high = cubed.astype(bf16)
        low = (cubed - high.astype(f32)).astype(bf16)
        highs[slot, u] = high
        lows[slot, u] = low
        highs_turned[slot, u] = jnp.transpose(high)
        lows_turned[slot, u] = jnp.transpose(low)

    def use_one(buffer, sender, group, slot, u):
        k = group * GROUP + u
        near_at = partner_of(sender, k)
        block = buffer[sender, LINES * k : LINES * k + LINES]
        high, low = highs[slot, u], lows[slot, u]
        own_charge = charge[near_at]
        sums = dot(own_charge, high, (1, 0))
        sums = sums[0:16] + sums[16:32] + dot(own_charge[0:16], low, (1, 0))
        valid = jnp.clip(partner_smem[sender, k] + 1, 0, 1).astype(f32)
        rows = force_rows(block, sums) * valid
        for l in range(3):
            back[sender, l, k : k + 1] = rows[l : l + 1]
        far_charge = charge_features(block)
        sums = dot(far_charge, highs_turned[slot, u], (1, 0))
        sums = sums[0:16] + sums[16:32] + dot(far_charge[0:16], lows_turned[slot, u], (1, 0))
        rows = force_rows(own_block(near_at), sums)
        for l in range(3):
            near[l, sender, k : k + 1] = rows[l : l + 1]

    def advance(later, now, slot):
        for u in range(GROUP):
            if later is not None:
                compute_one(*later, 1 - slot, u)
            if now is not None:
                use_one(*now, slot, u)

    columns = lax.broadcasted_iota(i32, (blocks, 128), 1)
    moments = jnp.zeros((blocks, 128), f32)
    terms = q + [q[c] * x[l] for c in range(3) for l in range(3)]
    for m, term in enumerate(terms):
        moments = jnp.where(columns == m, jnp.sum(term, axis=1, keepdims=True), moments)
    moments = moments * MOMENT_UNIT
    cells = n_col * share
    cell_hot = jnp.where(row_ids((cells, blocks)) == parent_block[...], 1.0, 0.0).astype(bf16)
    cell_part = hot_dot(cell_hot, moments)
    cell_sent[...] = cell_part.reshape(n_col, share, 128)
    cell_got[me] = cell_sent[me]
    top_hot = jnp.where(row_ids((C2, cells)) == parent_cell[...], 1.0, 0.0).astype(bf16)
    top_part = hot_dot(top_hot, cell_part)
    padded = jnp.concatenate([top_part, jnp.zeros((128 - C2, 128), f32)], axis=0)
    top_sent[...] = jnp.transpose(padded)[0:16]
    top_got[me] = top_sent[...]

    def moment_step(step, carry):
        peer = lax.rem(me + n_col - step, n_col)
        cell_copy(peer, me).start()
        top_copy(peer, me).start()
        return carry

    lax.fori_loop(1, n_col, moment_step, 0)

    def sum_of(got, count):
        total = got[0]
        for at in range(1, count):
            total = total + got[at]
        return total

    half = groups // 2
    base = groups - 1
    advance((sent, me, half), None, (base - half) % 2)
    for group in range(half, groups - 1):
        advance((sent, me, group + 1), (sent, me, group), (base - group + 1) % 2)

    first = source(codes)
    arrival(first).wait_recv()
    advance((received, first, 0), (sent, me, groups - 1), 1)

    def sum_tops():
        def wait_moments(step, carry):
            peer = lax.rem(me + step, n_col)
            cell_copy(peer, peer).wait_recv()
            top_copy(peer, peer).wait_recv()
            return carry

        lax.fori_loop(1, n_col, wait_moments, 0)
        row_sent[...] = sum_of(top_got, n_col)
        row_got[my_row] = row_sent[...]

        def row_step(step, carry):
            row_copy(lax.rem(my_row + step, n_row), my_row).start()
            return carry

        lax.fori_loop(1, n_row, row_step, 0)

    def sender_step(step, carry):
        code, send_code = carry[0:2], carry[2:4]
        sender = source(code)
        following_code = next_code(code)
        following = source(following_code)

        @pl.when(step + AHEAD < n_col - 1)
        def _():
            send_step(step, send_code)

        @pl.when(step == n_col // 2)
        def _():
            sum_tops()

        for group in range(groups - 1):
            advance((received, sender, group + 1), (received, sender, group), group % 2)
            start_back(sender, group)
        arrival(following).wait_recv()
        advance((received, following, 0), (received, sender, groups - 1), (groups - 1) % 2)
        start_back(sender, groups - 1)
        return following_code + next_code(send_code)

    lax.fori_loop(0, n_col - 1, sender_step, codes + send_code)

    for group in range(half):
        later = (received, me, group + 1) if group + 1 < half else None
        advance(later, (received, me, group), group % 2)
    cell_sum = sum_of(cell_got, n_col)
    cell_rows = jnp.concatenate([cell_sum, jnp.zeros((128 - share, 128), f32)], axis=0)
    cell_out[...] = jnp.transpose(cell_rows)[0:12, 0:share]

    returned[me] = back[me]

    def row_wait(other, carry):
        peer = lax.rem(my_row + other, n_row)
        row_copy(peer, peer).wait_recv()
        return carry

    lax.fori_loop(1, n_row, row_wait, 0)
    top_out[...] = sum_of(row_got, n_row)[0:12, 0:C2]

    pairs = n_col * slots
    pair = lax.broadcasted_iota(i32, (slots, pairs), 1)
    pair_row = row_ids((slots, pairs))
    in_slot = jnp.where(lax.rem(pair, slots) == pair_row, 1.0, 0.0).astype(bf16)
    pair_c = lax.broadcasted_iota(i32, (n_col, pairs), 1)
    in_peer = jnp.where(lax.div(pair_c, slots) == row_ids((n_col, pairs)), 1.0, 0.0)
    block_id = row_ids((blocks, pairs)).astype(f32)

    def hot_of(listed):
        spread = dot(listed[...].astype(f32).astype(bf16), in_slot, (1, 0))
        flat = jnp.sum(spread * in_peer, axis=0, keepdims=True)
        return jnp.where(block_id == flat, 1.0, 0.0).astype(bf16)

    near_hot = hot_of(partner_vmem)
    totals = [hot_dot(near_hot, near[l].reshape(pairs, width)) for l in range(3)]
    sent_hot = hot_of(send_vmem)

    def finish(step, carry):
        peer = lax.rem(me + step, n_col)
        back_arrival(peer).wait_recv()
        return carry

    lax.fori_loop(1, n_col, finish, 0)
    for l in range(3):
        force[l] = totals[l] + hot_dot(sent_hot, returned[:, l].reshape(pairs, width))

    def drain(step, carry):
        peer = lax.rem(me + step, n_col)
        send_copy(peer).wait_send()
        back_copy(peer).wait_send()
        cell_copy(peer, me).wait_send()
        top_copy(peer, me).wait_send()
        return carry

    lax.fori_loop(1, n_col, drain, 0)

    def drain_row(step, carry):
        row_copy(lax.rem(my_row + step, n_row), my_row).wait_send()
        return carry

    lax.fori_loop(1, n_row, drain_row, 0)


def body(positions, strengths, live_count, send_list, partner, parent_block, parent_cell):
    n_row, n_col = lax.axis_size("row"), lax.axis_size("col")
    blocks, width = positions.shape[2:]
    slots = send_list.shape[3]
    cells = parent_cell.shape[1]
    share = cells // n_col
    vmem = pl.BlockSpec(memory_space=pltpu.VMEM)
    hbm = pl.BlockSpec(memory_space=pltpu.HBM)
    dma = pltpu.SemaphoreType.DMA
    force, cell, top = pl.pallas_call(
        functools.partial(kernel, n_row, n_col, slots),
        out_shape=(
            jax.ShapeDtypeStruct((3, blocks, width), f32),
            jax.ShapeDtypeStruct((12, share), f32),
            jax.ShapeDtypeStruct((12, C2), f32),
        ),
        in_specs=[hbm] * 7,
        out_specs=(vmem, vmem, vmem),
        scratch_shapes=[
            pltpu.VMEM((3, blocks, width), f32),
            pltpu.VMEM((3, blocks, width), f32),
            pltpu.VMEM((1, blocks), i32),
            pltpu.SMEM((n_col, slots), i32),
            pltpu.SMEM((n_col, slots), i32),
            pltpu.VMEM((n_col, slots), i32),
            pltpu.VMEM((n_col, slots), i32),
            pltpu.VMEM((1, blocks), i32),
            pltpu.VMEM((1, cells), i32),
            pltpu.VMEM((width // 128, blocks * 8, 128), f32),
            pltpu.VMEM((blocks, 8, width), f32),
            pltpu.VMEM((blocks, width, 48), bf16),
            pltpu.VMEM((blocks, 32, width), bf16),
            pltpu.VMEM((n_col, slots * LINES, width), f32),
            pltpu.VMEM((n_col, slots * LINES, width), f32),
            pltpu.VMEM((n_col, 3, slots, width), f32),
            pltpu.VMEM((n_col, 3, slots, width), f32),
            pltpu.VMEM((3, n_col, slots, width), f32),
            pltpu.VMEM((2, GROUP, width, width), bf16),
            pltpu.VMEM((2, GROUP, width, width), bf16),
            pltpu.VMEM((2, GROUP, width, width), bf16),
            pltpu.VMEM((2, GROUP, width, width), bf16),
            pltpu.VMEM((n_col, share, 128), f32),
            pltpu.VMEM((n_col, share, 128), f32),
            pltpu.VMEM((16, 128), f32),
            pltpu.VMEM((n_col, 16, 128), f32),
            pltpu.VMEM((16, 128), f32),
            pltpu.VMEM((n_row, 16, 128), f32),
            *[dma((n_col,)) for _ in range(8)],
            dma((n_row,)),
            dma((n_row,)),
            dma((9,)),
        ],
        compiler_params=pltpu.CompilerParams(
            collective_id=0, has_side_effects=True, vmem_limit_bytes=40 * 1024 * 1024
        ),
        name="pair_forces",
    )(*[
        pltpu.with_memory_space_constraint(each, pltpu.HBM)
        for each in (
            positions[:, 0], strengths[:, 0], live_count, send_list[0, 0], partner[0, 0], parent_block, parent_cell
        )
    ])
    return force[:, None], cell[:, None, :], top


def solution(mesh):
    placed = (
        P(None, "row", "col", None),
        P(None, "row", "col", None),
        P("row", "col"),
        P("row", "col", None, None),
        P("row", "col", None, None),
        P("row", "col"),
        P("row", None),
    )
    return jax.shard_map(
        body,
        mesh=mesh,
        in_specs=placed,
        out_specs=(P(None, "row", "col", None), P(None, "row", "col"), P()),
        check_vma=False,
    )
```
